32 devices in a mesh: tok: 8 (over y, x, core), col: 4 (over z).
Axes of the slice: x: 2, y: 2, z: 4, core: 2. Of those that a mesh axis runs over, the one named last changes fastest.
Arguments:
- rollout: bfloat16 [1024, 5120], P('tok'), may hold values from -6 to 6
- lengths: int32 [16], P('tok'), may hold values from 16 to 64
- route: int32 [1024, 1], P('tok'), may hold values from 0 to 7; in each aligned block of 128 rows (0 to 127, 128 to 255, ...) at most 32 rows name the same one
- up_codes: bfloat16 [5120, 2048], P('tok', 'col'), may hold values from -4 to 4
- up_scales: float32 [20, 8], P(None, 'col'), may hold values from 0.0069877123 to 0.02795085
- block_rows: int32 [8, 2], P('col'), may hold values from 0 to 19, as said below
- delta: float32 [256, 8, 2, 256], P('tok', 'col'), may hold values from -0.125 to 0.125
- adam_m: float32 [256, 8, 2, 256], P('tok', 'col'), may hold values from -12 to 12
- adam_v: float32 [256, 8, 2, 256], P('tok', 'col'), may hold values from 1 to 30
- gate_pre: bfloat16 [2048, 2048], P('tok', 'col'), may hold values from -8 to 8
- hidden_grad: bfloat16 [2048, 2048], P('tok', 'col'), may hold values from -0.875 to 0.875
Outputs:
- input_grad: bfloat16 [2048, 5120], P('tok', 'col')
- gate_grad: bfloat16 [2048, 2048], P('tok', 'col')
- new_delta: float32 [256, 8, 2, 256], P('tok', 'col')
- new_m: float32 [256, 8, 2, 256], P('tok', 'col')
- new_v: float32 [256, 8, 2, 256], P('tok', 'col')
- delta_scale: float32 [8, 2], P('col')
- delta_codes: bfloat16 [256, 8, 2, 256], P('tok', 'col')
The draws below stay inside these ranges and needn't reach their ends.
Inputs may be any that keep to these rules, and one draw needn't show every extreme that they name: `route`: at most 32 of the 128 rows of one index of tok name the same learner shard, and some learner shard is named by exactly 32 of them. `block_rows`: the 2 row blocks of one column block are distinct.
All inputs are finite; a program needn't handle non-finite values. Where the reference program divides by a largest or mean magnitude, that divisor is 1e-20 or more.
Results may differ from the reference program's by a relative error of at most 0.017.
Values may be sent and summed in bfloat16 or wider, within the bound.
No kernel may reach another device: no remote copies, remote signals or barrier semaphores. Data moves between devices by JAX's collectives and lax.ppermute only.
A program may use at most 128 MiB of HBM per device.

```python
import math
import jax
import jax.numpy as jnp
import numpy as np
from jax import lax

D = 5120
BLK = 256
K = 2
RESP = 64
STEP = 1000
TOK_DEV = 128
SEND = 1024
SEQS = 16
CAP = 32
LROWS = 256
LEARN = 2048
FFB = 8
FF = 2048
DB = 20
N_TOK = 8
N_COL = 4


def draw_block_rows(key, part):
    key = jax.random.fold_in(key, 7)
    scores = jax.random.randint(key, (FFB, DB), 0, 65536) * DB + jnp.arange(DB, dtype=jnp.int32)[None, :]
    return lax.top_k(scores, K)[1].astype(jnp.int32)


def place_ends(result, rng, smallest, top_value):
    spot = [jax.random.randint(jax.random.fold_in(rng, axis), (), 0, length) for axis, length in enumerate(result.shape)]
    longest = result.shape.index(max(result.shape))
    next_to = spot[:longest] + [(spot[longest] + 1) % result.shape[longest]] + spot[longest + 1:]
    return result.at[tuple(spot)].set(smallest).at[tuple(next_to)].set(top_value)


def steps_of(stream_key, dims, cuts, low, top_value):
    def one(dim, shards_of):
        draws = jax.random.uniform(jax.random.fold_in(jax.random.fold_in(stream_key, 6), dim), (shards_of,), jnp.float32, low / len(cuts), top_value / len(cuts))
        return jnp.repeat(jnp.exp(draws), dims[dim] // shards_of).reshape((-1,) + (1,) * (len(dims) - dim - 1))

    factor_of = one(*cuts[0])
    for cut in cuts[1:]:
        factor_of = factor_of * one(*cut)
    return factor_of


def assign_block(stream_key, own, number, rows, number_of, top, bound, skew):
    sequence = jax.random.permutation(stream_key, number_of)
    heavy_load, ordinary = portions_of(number_of, rows * top, bound, skew, True), portions_of(number_of, rows * top, bound, skew, False)
    places = jnp.arange(number_of)

    def named(sizes, offset_by):
        used = int((sizes > 0).sum())
        fixed = max(1, used // 4)
        moved = fixed + (places - fixed + offset_by * (used - fixed)) % max(1, number_of - fixed)
        return jnp.zeros((number_of,), jnp.int32).at[sequence[jnp.where(places < fixed, places, moved)]].set(jnp.asarray(sizes, jnp.int32))

    sizes = jnp.where(number % 4 == 0, named(heavy_load, number // 4), named(ordinary, number - number // 4 - 1))
    mixed = jax.random.permutation(jax.random.fold_in(own, 3), number_of)
    giver, receiver = mixed[0:number_of // 2 * 2:2], mixed[1:number_of // 2 * 2:2]
    margin = jnp.minimum(sizes[giver] - 1, bound - sizes[receiver]) // 2
    margin = jnp.where((giver == sequence[0]) | (receiver == sequence[0]) | (sizes[receiver] == 0), 0, jnp.maximum(margin, 0))
    moved = jax.random.randint(jax.random.fold_in(own, 4), (number_of // 2,), 0, 1 << 20) % (margin + 1)
    sizes = sizes.at[giver].add(-moved).at[receiver].add(moved)
    items = jnp.searchsorted(jnp.cumsum(sizes), jnp.arange(rows * top), side="right").astype(jnp.int32)
    listing = items.reshape(top, rows).T
    listing = listing[jax.random.permutation(jax.random.fold_in(own, 1), rows)]
    offset_by = jax.random.randint(jax.random.fold_in(own, 2), (rows, 1), 0, top)
    return jnp.take_along_axis(listing, (jnp.arange(top)[None, :] + offset_by) % top, axis=1)


def portions_of(amount, total, most, lean, full):
    portions = [(1 << 20) // math.isqrt(standing ** lean) + 1 for standing in range(1, amount + 1)]
    largest = most if full else min(most, max(-(-total // amount), total * portions[0] // sum(portions)))
    least = 1 if total - largest >= amount - 1 else 0
    given, spare = [largest] + [least] * (amount - 1), total - largest - least * (amount - 1)
    while spare > 0:
        candidates = [i for i in range(1, amount) if given[i] < largest] or [i for i in range(1, amount) if given[i] < most]
        whole, remaining = sum([portions[i] for i in candidates]), spare
        for i in candidates:
            addition = min(most - given[i], max(1, remaining * portions[i] // whole), spare)
            given[i] = given[i] + addition
            spare = spare - addition
    return np.array(given)


def scatter_about(stream_key, dims, scale, bound, shards=(), kind=jnp.bfloat16):
    array = jax.random.normal(stream_key, dims, jnp.float32) * scale
    if len(shards) > 0:
        array = steps_of(stream_key, dims, shards, -0.22, 0.18) * array
    return jnp.clip(array, min=-bound, max=bound).astype(kind)


def setup_inputs(seed: int = 0) -> dict:
    splits = jax.random.split(jax.random.key(seed), 12)
    rollout = scatter_about(splits[0], (SEND, D), 1.0, 6.0, ((0, 8),))
    lengths = place_ends(jax.random.randint(splits[1], (SEQS,), RESP // 4, RESP + 1), jax.random.fold_in(splits[1], 1), RESP // 4, RESP).astype(jnp.int32)
    route_keys = jax.random.split(jax.random.fold_in(splits[2], 1), SEND // TOK_DEV)
    route_turns = jax.random.permutation(jax.random.fold_in(splits[2], 3), SEND // TOK_DEV)
    route = jax.vmap(lambda own, number: assign_block(jax.random.fold_in(splits[2], 2), own, number, TOK_DEV, N_TOK, 1, CAP, 2))(route_keys, route_turns).reshape((SEND, 1))
    up_codes = scatter_about(splits[3], (D, FF), 1.0, 4.0, ((0, 8), (1, 4)))
    up_scales = jnp.clip(jnp.exp(math.log(0.02795085) - 1.3862944 * jax.random.uniform(splits[4], (DB, FFB), jnp.float32) ** steps_of(splits[4], (DB, FFB), ((1, 4),), -0.2, 0.2)), 0.0069877123, 0.02795085)
    block_rows = draw_block_rows(jax.random.fold_in(splits[11], 71), 0)
    delta = scatter_about(splits[6], (BLK, FFB, K, BLK), (0.5 * (K * BLK) ** -0.5), 0.125, ((0, 8), (1, 4)), jnp.float32)
    adam_m = scatter_about(splits[7], (BLK, FFB, K, BLK), 2.0, 12.0, ((0, 8), (1, 4)), jnp.float32)
    adam_v = jnp.clip(jnp.exp(math.log(30.0) - 3.4011974 * jax.random.uniform(splits[8], (BLK, FFB, K, BLK), jnp.float32) ** steps_of(splits[8], (BLK, FFB, K, BLK), ((0, 8), (1, 4)), -0.2, 0.2)), 1.0, 30.0)
    gate_pre = scatter_about(splits[9], (LEARN, FF), 1.5, 8.0, ((0, 8), (1, 4)))
    hidden_grad = scatter_about(splits[10], (LEARN, FF), 0.15, 0.875, ((0, 8), (1, 4)))
    return dict(rollout=rollout, lengths=lengths, route=route, up_codes=up_codes, up_scales=up_scales, block_rows=block_rows, delta=delta, adam_m=adam_m, adam_v=adam_v, gate_pre=gate_pre, hidden_grad=hidden_grad)


beta_first = 0.9
beta_second = 0.999
step_rate = 0.01
adam_eps = 1e-08
scale_eps = 1e-06

def silu_slope(operand):
    sigmoid_value = jax.nn.sigmoid(operand)
    return sigmoid_value * (1.0 + operand * (1.0 - sigmoid_value))

def reference(rollout, lengths, route, up_codes, up_scales, block_rows, delta, adam_m, adam_v, gate_pre, hidden_grad):
    row_ids = jnp.arange(SEND, dtype=jnp.int32)
    seq_len = jnp.repeat(lengths, RESP)
    position = row_ids % RESP
    row_weight = jnp.where(position < seq_len, RESP / seq_len.astype(jnp.float32), 0.0).astype(jnp.float32)
    destination = route[:, 0]
    onehot = (destination[:, None] == jnp.arange(N_TOK, dtype=jnp.int32)[None, :]).astype(jnp.int32)
    ranks = jnp.cumsum(onehot.reshape(N_TOK, TOK_DEV, N_TOK), axis=1).reshape(SEND, N_TOK) - 1
    slot_index = lax.optimization_barrier(jnp.sum(ranks * onehot, axis=1)).astype(jnp.int32)
    target = (destination * LROWS + row_ids // TOK_DEV * CAP + slot_index).astype(jnp.int32)
    learn_x = jnp.zeros((LEARN, D), jnp.bfloat16).at[target].set(rollout)
    learn_w = jnp.zeros((LEARN,), jnp.float32).at[target].set(row_weight)
    scale_full = jnp.repeat(jnp.repeat(up_scales, BLK, axis=0), BLK, axis=1)
    up_weight = (up_codes.astype(jnp.float32) * scale_full).astype(jnp.bfloat16)
    delta_half = delta.astype(jnp.bfloat16)
    chosen = jnp.take(learn_x.reshape(LEARN, DB, BLK), block_rows.reshape(-1), axis=1).reshape(LEARN, FFB, K, BLK)
    activation = jax.nn.silu(gate_pre.astype(jnp.float32))
    up_grad = (hidden_grad.astype(jnp.float32) * activation * learn_w[:, None]).astype(jnp.bfloat16)
    up_grad_blocks = up_grad.reshape(LEARN, FFB, BLK)
    delta_up = jnp.einsum('rjkb,bjkc->rjc', chosen.astype(jnp.float32), delta_half.astype(jnp.float32)).reshape(LEARN, FF)
    up_value = jnp.dot(learn_x, up_weight, preferred_element_type=jnp.float32) + delta_up
    gate_grad = (hidden_grad.astype(jnp.float32) * up_value * silu_slope(gate_pre.astype(jnp.float32)) * learn_w[:, None]).astype(jnp.bfloat16)
    delta_back = jnp.einsum('rjc,bjkc->rjkb', up_grad_blocks.astype(jnp.float32), delta_half.astype(jnp.float32))
    group_blocks = FFB // N_COL
    group_width = FF // N_COL

    def add_group(summed, group_index):
        first_column = group_index * group_width
        grad_part = lax.dynamic_slice_in_dim(up_grad, first_column, group_width, 1)
        weight_part = lax.dynamic_slice_in_dim(up_weight, first_column, group_width, 1)
        partial_sum = lax.dot_general(grad_part, weight_part, (((1,), (1,)), ((), ())), preferred_element_type=jnp.float32)
        back_part = lax.dynamic_slice_in_dim(delta_back, group_index * group_blocks, group_blocks, 1).reshape(LEARN, group_blocks * K, BLK)
        rows_part = lax.dynamic_slice_in_dim(block_rows, group_index * group_blocks, group_blocks, 0).reshape(-1)
        placed = jnp.zeros((LEARN, DB, BLK), jnp.float32).at[:, rows_part].add(back_part)
        partial_sum = partial_sum + placed.reshape(LEARN, D)
        return (summed + partial_sum, None)
    summed = lax.scan(add_group, jnp.zeros((LEARN, D), jnp.float32), jnp.arange(N_COL, dtype=jnp.int32))[0]
    input_grad = summed.astype(jnp.bfloat16)
    gradient = jnp.einsum('rjkb,rjc->bjkc', chosen.astype(jnp.float32), up_grad_blocks.astype(jnp.float32))
    new_m = beta_first * adam_m + (1.0 - beta_first) * gradient
    new_v = beta_second * adam_v + (1.0 - beta_second) * gradient * gradient
    corrected_m = new_m / (1.0 - beta_first ** STEP)
    corrected_v = new_v / (1.0 - beta_second ** STEP)
    new_delta = delta - step_rate * corrected_m / (jnp.sqrt(corrected_v) + adam_eps)
    delta_scale = lax.optimization_barrier(jnp.max(jnp.abs(new_delta), axis=(0, 3)))
    delta_codes = (new_delta / (delta_scale + scale_eps)[None, :, :, None]).astype(jnp.bfloat16)
    return (input_grad, gate_grad, new_delta, new_m, new_v, delta_scale, delta_codes)
```

```python
import functools

import jax
import jax.numpy as jnp
from jax import lax
from jax.experimental import pallas as pl
from jax.experimental.pallas import tpu as pltpu
from jax.sharding import PartitionSpec as P

BLK = 256
K = 2
RESP = 64
STEP = 1000


beta_first = 0.9
beta_second = 0.999
step_rate = 0.01
adam_eps = 1e-08
scale_eps = 1e-06


def silu_slope(operand):
    sigmoid_value = jax.nn.sigmoid(operand)
    return sigmoid_value * (1.0 + operand * (1.0 - sigmoid_value))


def dequant(code_rows, scales):
    row_count = code_rows.shape[0]
    block_count = scales.shape[0]
    width_blocks = scales.shape[1]
    block_of_row = jnp.arange(row_count, dtype=jnp.int32) // BLK
    selector = (block_of_row[:, None] == jnp.arange(block_count, dtype=jnp.int32)[None, :]).astype(
        jnp.float32
    )
    row_scales = jnp.dot(selector, scales, precision=lax.Precision.HIGHEST)
    spread = (
        code_rows.astype(jnp.float32).reshape(row_count, width_blocks, -1) * row_scales[:, :, None]
    )
    return spread.reshape(row_count, -1).astype(jnp.bfloat16)


def any_mesh(
    rollout,
    lengths,
    route,
    up_codes,
    up_scales,
    block_rows,
    delta,
    adam_m,
    adam_v,
    gate_pre,
    hidden_grad,
):
    peer_count = lax.axis_size("tok")
    send_rows = rollout.shape[0]
    row_width = rollout.shape[1]
    capacity = 2 * send_rows // peer_count
    row_ids = jnp.arange(send_rows, dtype=jnp.int32)
    seq_len = jnp.repeat(lengths, RESP)
    position = row_ids % RESP
    row_weight = jnp.where(position < seq_len, RESP / seq_len.astype(jnp.float32), 0.0)
    destination = route[:, 0]
    onehot = (destination[:, None] == jnp.arange(peer_count, dtype=jnp.int32)[None, :]).astype(
        jnp.int32
    )
    slot_index = jnp.sum((jnp.cumsum(onehot, axis=0) - 1) * onehot, axis=1)
    target = destination * capacity + slot_index
    weight_slots = (
        jnp.zeros((peer_count * capacity,), jnp.float32)
        .at[target]
        .set(row_weight)
        .reshape(peer_count, capacity)
    )
    buffer = (
        jnp.zeros((peer_count * capacity, row_width), jnp.bfloat16)
        .at[target]
        .set(rollout)
        .reshape(peer_count, capacity, row_width)
    )
    arrived, arrived_weight = (
        lax.all_to_all(buffer, "tok", split_axis=0, concat_axis=0, tiled=True),
        lax.all_to_all(
            weight_slots.astype(jnp.bfloat16), "tok", split_axis=0, concat_axis=0, tiled=True
        ).astype(weight_slots.dtype),
    )
    learn_x = arrived.reshape(peer_count * capacity, row_width)
    learn_w = arrived_weight.reshape(peer_count * capacity)
    rows_learn = learn_x.shape[0]
    column_count = up_codes.shape[1]
    blocks_here = column_count // BLK
    block_total = up_scales.shape[0]
    delta_full = lax.all_gather(delta.astype(jnp.bfloat16), "tok", axis=0, tiled=True)
    chosen = jnp.take(
        learn_x.reshape(rows_learn, block_total, BLK), block_rows.reshape(-1), axis=1
    ).reshape(rows_learn, blocks_here, K, BLK)
    activation = jax.nn.silu(gate_pre.astype(jnp.float32))
    up_grad = (hidden_grad.astype(jnp.float32) * activation * learn_w[:, None]).astype(jnp.bfloat16)
    up_grad_blocks = up_grad.reshape(rows_learn, blocks_here, BLK)
    delta_up = jnp.einsum(
        "rjkb,bjkc->rjc", chosen, delta_full, preferred_element_type=jnp.float32
    ).reshape(rows_learn, column_count)
    delta_back = jnp.einsum(
        "rjc,bjkc->rjkb", up_grad_blocks, delta_full, preferred_element_type=jnp.float32
    )
    selector = (
        block_rows.reshape(-1)[:, None] == jnp.arange(block_total, dtype=jnp.int32)[None, :]
    ).astype(jnp.float32)
    delta_input = jnp.einsum(
        "rqb,qd->rdb",
        delta_back.reshape(rows_learn, -1, BLK),
        selector,
        precision=lax.Precision.HIGHEST,
    ).reshape(rows_learn, row_width)
    weight = dequant(lax.all_gather(up_codes, "tok", axis=0, tiled=True), up_scales)
    base_up = jnp.dot(learn_x, weight, preferred_element_type=jnp.float32)
    weight = dequant(lax.all_gather(up_codes, "tok", axis=0, tiled=True), up_scales)
    base_input = lax.dot_general(
        up_grad, weight, (((1,), (1,)), ((), ())), preferred_element_type=jnp.float32
    )
    up_value = base_up + delta_up
    gate_grad = (
        hidden_grad.astype(jnp.float32)
        * up_value
        * silu_slope(gate_pre.astype(jnp.float32))
        * learn_w[:, None]
    ).astype(jnp.bfloat16)
    input_grad = lax.psum_scatter(
        base_input + delta_input, "col", scatter_dimension=1, tiled=True
    ).astype(jnp.bfloat16)
    owned_rows = BLK // peer_count
    summed_grad = lax.psum(
        jnp.einsum("rjkb,rjc->bjkc", chosen, up_grad_blocks, preferred_element_type=jnp.float32),
        "tok",
    )
    gradient = lax.dynamic_slice_in_dim(
        summed_grad, lax.axis_index("tok") * owned_rows, owned_rows, 0
    )
    new_m = beta_first * adam_m + (1.0 - beta_first) * gradient
    new_v = beta_second * adam_v + (1.0 - beta_second) * gradient * gradient
    corrected_m = new_m / (1.0 - beta_first**STEP)
    corrected_v = new_v / (1.0 - beta_second**STEP)
    new_delta = delta - step_rate * corrected_m / (jnp.sqrt(corrected_v) + adam_eps)
    local_max = jnp.max(jnp.abs(new_delta), axis=(0, 3))
    block_scale = lax.pmax(local_max, "tok")
    new_codes = (new_delta / (block_scale + scale_eps)[None, :, :, None]).astype(jnp.bfloat16)
    return (input_grad, gate_grad, new_delta, new_m, new_v, block_scale, new_codes)


LANE = 128
META = 16
FAST_LIMIT = 64 * 1024 * 1024


def call(kernel, out_shape, flops=0, moved=0, **extra):
    return pl.pallas_call(
        kernel,
        out_shape=out_shape,
        compiler_params=pltpu.CompilerParams(vmem_limit_bytes=FAST_LIMIT),
        cost_estimate=pl.CostEstimate(flops=flops, bytes_accessed=moved, transcendentals=0),
        **extra,
    )


VMEM = pl.BlockSpec(memory_space=pltpu.VMEM)
SMEM = pl.BlockSpec(memory_space=pltpu.SMEM)
HBM = pl.BlockSpec(memory_space=pltpu.HBM)
AFTER = pl.BlockSpec(memory_space=pl.ANY)


def own_place():
    token = lax.axis_index("tok")
    return token & 1, lax.shift_right_logical(token, 1)


def fetch(pairs, sems):
    copies = [pltpu.make_async_copy(*pair, sems.at[n]) for n, pair in enumerate(pairs)]
    for copy in copies:
        copy.start()
    return copies


def learner_kernel(gate_hbm, hidden_hbm, delta_hbm, out_ref, gate_ref, hidden_ref, delta_ref, sems):
    copies = fetch([(gate_hbm, gate_ref), (hidden_hbm, hidden_ref), (delta_hbm, delta_ref)], sems)
    peers, _, width = out_ref.shape
    cap = gate_ref.shape[0] // peers
    owned = delta_ref.shape[0]
    copies[0].wait()
    copies[1].wait()
    gate = gate_ref[...].astype(jnp.float32)
    raw = hidden_ref[...].astype(jnp.float32) * gate / (1.0 + jnp.exp(-gate))
    out_ref[:, :cap, :] = raw.astype(jnp.bfloat16).reshape(peers, cap, width)
    copies[2].wait()
    for j in range(delta_ref.shape[1]):
        for k in range(K):
            half = delta_ref[:, j, k, :].astype(jnp.bfloat16)
            for peer in range(k, peers, K):
                out_ref[peer, cap:, j * BLK : (j + 1) * BLK] = half


def place_matrix(target_row, slots):
    rows = target_row.shape[1]
    ids = lax.broadcasted_iota(jnp.int32, (slots, rows), 0)
    return (ids == target_row).astype(jnp.bfloat16)


def as_column(row):
    size = row.shape[1]
    first = lax.broadcasted_iota(jnp.int32, (size, size), 0)
    second = lax.broadcasted_iota(jnp.int32, (size, size), 1)
    return jnp.sum(jnp.where(first == second, row, 0.0), axis=1, keepdims=True)


def weight_of(length_row):
    position = lax.rem(lax.broadcasted_iota(jnp.int32, length_row.shape, 1), RESP)
    return jnp.where(position.astype(jnp.float32) < length_row, RESP / length_row, 0.0)


def sender_kernel(lengths_ref, route_ref, arrived_hbm, out_ref, raw_ref, delta_ref, sems):
    peers, cap, width = raw_ref.shape
    rows = route_ref.shape[1]
    copies = fetch([(arrived_hbm.at[:, :cap, :], raw_ref), (arrived_hbm.at[:, cap:, :], delta_ref)], sems)
    route = route_ref[...]
    named = (lax.broadcasted_iota(jnp.int32, (max(peers, 16), rows), 0) == route).astype(jnp.float32)
    before = (
        lax.broadcasted_iota(jnp.int32, (rows, rows), 0)
        < lax.broadcasted_iota(jnp.int32, (rows, rows), 1)
    ).astype(jnp.bfloat16)
    ranks = jnp.dot(named.astype(jnp.bfloat16), before, preferred_element_type=jnp.float32)
    slot = jnp.sum(named * ranks, axis=0, keepdims=True).astype(jnp.int32)
    target = route * cap + slot
    row_ids = lax.broadcasted_iota(jnp.int32, (1, rows), 1)
    length_row = jnp.zeros((1, rows), jnp.float32)
    for seq in range(rows // RESP):
        mine = (row_ids >= seq * RESP) & (row_ids < (seq + 1) * RESP)
        length_row = jnp.where(mine, lengths_ref[seq].astype(jnp.float32), length_row)
    place = place_matrix(target, peers * cap)
    copies[0].wait()
    raw = raw_ref[...].reshape(peers * cap, width)
    picked = lax.dot_general(
        place, raw, (((0,), (0,)), ((), ())), preferred_element_type=jnp.float32
    )
    out_ref[:rows, :] = (picked * as_column(weight_of(length_row))).astype(jnp.bfloat16)
    out_ref[rows : rows + META, :] = jnp.zeros((META, width), jnp.bfloat16)
    meta_ids = lax.broadcasted_iota(jnp.int32, (META, rows), 0)
    meta = jnp.where(meta_ids == 0, target.astype(jnp.float32), 0.0)
    meta = jnp.where(meta_ids == 1, length_row, meta)
    out_ref[rows : rows + META, :rows] = meta.astype(jnp.bfloat16)
    copies[1].wait()
    out_ref[rows + META :, :] = delta_ref[...].reshape(-1, width)


def gradient_kernel(rows_ref, own_x, mate_x, own_up, mate_up, *refs):
    out_refs, (held_ref, x_ref, up_ref, sems) = refs[:-4], refs[-4:]
    chips, spots, owned, width = held_ref.shape
    rows = own_x.shape[0]
    pairs = []
    for seat, (x_hbm, up_hbm) in enumerate(((own_x, own_up), (mate_x, mate_up))):
        lines = slice(seat * rows, (seat + 1) * rows)
        pairs.append((up_hbm.at[:rows, :], up_ref.at[lines]))
        for spot in range(spots):
            lanes = pl.ds(pl.multiple_of(rows_ref[spot // K, spot % K] * BLK, BLK), BLK)
            pairs.append((x_hbm.at[:, lanes], x_ref.at[spot, lines]))
    for copy in fetch(pairs, sems):
        copy.wait()
    core, own_chip = own_place()
    for spot in range(spots):
        j = spot // K
        full = lax.dot_general(
            x_ref[spot],
            up_ref[:, j * BLK : (j + 1) * BLK],
            (((0,), (0,)), ((), ())),
            preferred_element_type=jnp.float32,
        ).reshape(chips, 2, owned, width)
        held_ref[:, spot] = jnp.where(core == 0, full[:, 0], full[:, 1]).astype(jnp.bfloat16)
    for distance, out_ref in enumerate(out_refs):
        out_ref[...] = held_ref[own_chip ^ distance]


def adam_kernel(delta_hbm, m_hbm, v_hbm, *refs):
    delta_out, m_out, v_out, max_out, delta_ref, m_ref, v_ref, grad_ref, sems = refs[-9:]
    chips = grad_ref.shape[0]
    pairs = [(delta_hbm, delta_ref), (m_hbm, m_ref), (v_hbm, v_ref)]
    for copy in fetch(pairs + [(refs[chip], grad_ref.at[chip]) for chip in range(chips)], sems):
        copy.wait()
    ids = lax.broadcasted_iota(jnp.int32, max_out.shape, 1)
    tops = jnp.zeros(max_out.shape, jnp.float32)
    for j in range(delta_ref.shape[1]):
        for k in range(K):
            spot = j * K + k
            gradient = grad_ref[0, spot].astype(jnp.float32)
            for chip in range(1, chips):
                gradient = gradient + grad_ref[chip, spot].astype(jnp.float32)
            new_m = beta_first * m_ref[:, j, k, :] + (1.0 - beta_first) * gradient
            new_v = beta_second * v_ref[:, j, k, :] + (1.0 - beta_second) * gradient * gradient
            corrected_m = new_m / (1.0 - beta_first**STEP)
            corrected_v = new_v / (1.0 - beta_second**STEP)
            new_delta = delta_ref[:, j, k, :] - step_rate * corrected_m / (
                jnp.sqrt(corrected_v) + adam_eps
            )
            m_out[:, j, k, :] = new_m
            v_out[:, j, k, :] = new_v
            delta_out[:, j, k, :] = new_delta
            tops = jnp.where(ids == spot, jnp.max(jnp.abs(new_delta)), tops)
    high = tops.astype(jnp.bfloat16).astype(jnp.float32)
    middle = (tops - high).astype(jnp.bfloat16).astype(jnp.float32)
    low = tops - high - middle
    kinds = lax.broadcasted_iota(jnp.int32, max_out.shape, 0)
    tops = jnp.where(kinds == 0, high, jnp.where(kinds == 1, middle, low))
    max_out[...] = jnp.where(kinds < 3, tops, 0.0).astype(jnp.bfloat16)


def block_order(core, step):
    return (0, 1 + core, 2 - core, 3)[step]


def product_kernel(scales_ref, rows_ref, own_up, mate_up, *refs, steps, rows):
    last = steps[-1] == 3
    codes_hbm, refs = refs[: len(steps)], refs[len(steps) :]
    if last:
        refs = refs[4:]
        weight_out, *back_refs = refs[:5]
    else:
        own_x, mate_x, sum_ref, *back_refs = refs[:7]
    codes, weight, up, delta, sems, *rest = refs[5 if last else 7 :]
    core, own_chip = own_place()
    turn = own_chip ^ lax.axis_index("col")
    size, width = weight.shape[1:]
    tiles = size // LANE
    pairs = []
    for seat, up_hbm in enumerate((own_up, mate_up)):
        pairs.append((up_hbm.at[:rows, :], up.at[seat * rows : (seat + 1) * rows]))
        pairs.append((up_hbm.at[rows + META :, :], delta.at[core ^ seat]))
    shared = len(pairs)
    each = 1 if last else 3
    starts = []
    for spot, step in enumerate(steps):
        first_tile = (2 * (own_chip ^ block_order(core, step)) + core) * tiles
        starts.append(first_tile)
        pairs.append((codes_hbm[spot], codes.at[spot]))
        if not last:
            lanes = pl.ds(pl.multiple_of(first_tile * LANE, LANE), size)
            pairs.append((own_x.at[:, lanes], rest[0].at[spot, :rows]))
            pairs.append((mate_x.at[:, lanes], rest[0].at[spot, rows:]))
    copies = fetch(pairs, sems)
    for spot, step in enumerate(steps):
        for copy in copies[shared + each * spot : shared + each * (spot + 1)]:
            copy.wait()
        for tile in range(tiles):
            block = lax.div(starts[spot] + tile, BLK // LANE)
            lines = slice(tile * LANE, (tile + 1) * LANE)
            for j in range(width // BLK):
                lanes = slice(j * BLK, (j + 1) * BLK)
                plain = codes[spot, lines, lanes].astype(jnp.float32) * scales_ref[j, block]
                weight[spot, lines, lanes] = plain.astype(jnp.bfloat16)
        if spot == 0:
            for copy in copies[:shared]:
                copy.wait()
        for j in range(width // BLK):
            lanes = slice(j * BLK, (j + 1) * BLK)
            for k in range(K):
                for piece in range(BLK // LANE):
                    tile = rows_ref[j, k] * (BLK // LANE) + piece - starts[spot]

                    @pl.when((tile >= 0) & (tile < tiles))
                    def _():
                        lines = pl.ds(pl.multiple_of(tile * LANE, LANE), LANE)
                        extra = delta[k, piece * LANE : (piece + 1) * LANE, lanes].astype(jnp.float32)
                        held = weight[spot, lines, lanes].astype(jnp.float32)
                        weight[spot, lines, lanes] = (held + extra).astype(jnp.bfloat16)

        back = lax.dot_general(
            up[...], weight[spot], (((1,), (1,)), ((), ())), preferred_element_type=jnp.float32
        ).astype(jnp.bfloat16)
        if last:
            rest[0][...] = back
            weight_copy = pltpu.make_async_copy(weight.at[spot], weight_out, rest[1].at[1])
            weight_copy.start()
        for shift, back_ref in enumerate(back_refs):

            @pl.when((turn ^ block_order(core, step)) == shift)
            def _():
                if last:
                    back_copy = pltpu.make_async_copy(rest[0], back_ref, rest[1].at[0])
                    back_copy.start()
                    back_copy.wait()
                else:
                    back_ref[...] = back

        if last:
            weight_copy.wait()
        elif spot == 0:
            sum_ref[...] = jnp.dot(rest[0][spot], weight[spot], preferred_element_type=jnp.float32)
        else:
            sum_ref[...] += jnp.dot(rest[0][spot], weight[spot], preferred_element_type=jnp.float32)


def products(steps, scales, block_rows, own_up, mate_up, codes, *more):
    size, width = codes[0].shape
    rows = own_up.shape[0] - META - BLK
    count = len(steps)
    last = steps[-1] == 3
    back = jax.ShapeDtypeStruct((2 * rows, size), jnp.bfloat16)
    if last:
        first = jax.ShapeDtypeStruct((size, width), jnp.bfloat16)
        rest = [pltpu.VMEM(back.shape, jnp.bfloat16), pltpu.SemaphoreType.DMA((2,))]
    else:
        first = jax.ShapeDtypeStruct((2 * rows, width), jnp.float32)
        rest = [pltpu.VMEM((count, 2 * rows, size), jnp.bfloat16)]
    return call(
        functools.partial(product_kernel, steps=steps, rows=rows),
        [first] + [back] * 4,
        in_specs=[SMEM] * 2 + [HBM] * (2 + count + len(more)),
        out_specs=[HBM if last else VMEM] * 5,
        scratch_shapes=[
            pltpu.VMEM((count, size, width), jnp.bfloat16),
            pltpu.VMEM((count, size, width), jnp.bfloat16),
            pltpu.VMEM((2 * rows, width), jnp.bfloat16),
            pltpu.VMEM((K, BLK, width), jnp.bfloat16),
            pltpu.SemaphoreType.DMA((4 + 3 * count,)),
        ]
        + rest,
        input_output_aliases={4 + count + n: 1 + n for n in range(4)} if last else {},
    )(scales, block_rows, own_up, mate_up, *codes, *more)


def forward_kernel(own_x, mate_x, weight_hbm, sum_hbm, own_out, mate_out, x, weight, total, sems):
    size = weight.shape[0]
    rows = own_out.shape[0]
    core, own_chip = own_place()
    lanes = pl.ds(pl.multiple_of((2 * (own_chip ^ 3) + core) * size, LANE), size)
    pairs = [(own_x.at[:, lanes], x.at[:rows]), (mate_x.at[:, lanes], x.at[rows:])]
    for copy in fetch(pairs + [(weight_hbm, weight), (sum_hbm, total)], sems):
        copy.wait()
    full = total[...] + jnp.dot(x[...], weight[...], preferred_element_type=jnp.float32)
    own_out[...] = full[:rows]
    mate_out[...] = full[rows:]


def spread_up_kernel(own_up, own_sum, other_sum, tops_ref, out_ref):
    peers, lines, _ = out_ref.shape
    rows, width = own_sum.shape
    cap, half = lines // 2, width // 2
    target = own_up[rows : rows + META, :rows].astype(jnp.float32)
    place = place_matrix(target[0:1].astype(jnp.int32), peers * cap)
    value = (own_sum[...] + other_sum[...]) * as_column(weight_of(target[1:2]))
    placed = jnp.dot(place, value.astype(jnp.bfloat16), preferred_element_type=jnp.float32)
    placed = placed.astype(jnp.bfloat16).reshape(peers, cap, width)
    for side in range(2):
        out_ref[:, side * cap : (side + 1) * cap, :half] = placed[:, :, side * half : (side + 1) * half]
    for peer in range(peers):
        out_ref[peer, :META, half:] = tops_ref[...]
        out_ref[peer, META:, half:] = jnp.zeros((lines - META, LANE), jnp.bfloat16)


def spread_kernel(own_up, mate_up, up_slots, *refs):
    parts_hbm, out_refs = refs[:4], refs[4:-4]
    held_ref, meta_ref, parts_ref, sems = refs[-4:]
    _, rows, size = parts_ref.shape
    rows = rows // 2
    peers = held_ref.shape[0]
    cap = 2 * rows // peers
    core, _ = own_place()
    token = lax.axis_index("tok")
    pairs = [(up.at[rows : rows + META, :rows], meta_ref.at[seat]) for seat, up in enumerate((own_up, mate_up))]
    pairs += [(part, parts_ref.at[n]) for n, part in enumerate(parts_hbm)]
    pairs += [(up_slots.at[token ^ d], far.at[:, size:]) for d, far in enumerate(out_refs)]
    copies = fetch(pairs, sems)
    for copy in copies[: 2 + len(parts_hbm)]:
        copy.wait()
    for seat in range(2):
        lines = slice(seat * rows, (seat + 1) * rows)
        summed = parts_ref[0, lines].astype(jnp.float32)
        for part in range(1, len(parts_hbm)):
            summed = summed + parts_ref[part, lines].astype(jnp.float32)
        target = meta_ref[seat].astype(jnp.float32)
        place = place_matrix(target[0:1].astype(jnp.int32), peers * cap)
        placed = jnp.dot(place, summed.astype(jnp.bfloat16), preferred_element_type=jnp.float32)
        start = pl.multiple_of((core ^ seat) * cap, cap)
        held_ref[:, pl.ds(start, cap), :] = placed.astype(jnp.bfloat16).reshape(peers, cap, size)
    for d, far_ref in enumerate(out_refs):
        far_ref[:, :size] = held_ref[token ^ d]
    for copy in copies[2 + len(parts_hbm) :]:
        copy.wait()


def finish_kernel(gate_hbm, hidden_hbm, delta_hbm, *refs):
    arrived_refs = refs[:-8]
    input_out, gate_out, scale_out, codes_out, gate_ref, hidden_ref, delta_ref, sems = refs[-8:]
    copies = fetch([(gate_hbm, gate_ref), (hidden_hbm, hidden_ref), (delta_hbm, delta_ref)], sems)
    size = input_out.shape[1] // 2
    cap = gate_ref.shape[0] // len(arrived_refs)
    half = gate_ref.shape[1] // 2
    token = lax.axis_index("tok")
    for distance, arrived_ref in enumerate(arrived_refs):
        sender = token ^ distance
        lines = pl.ds(pl.multiple_of((sender >> 1) * 2 * cap, 2 * cap), 2 * cap)
        lanes = pl.ds(pl.multiple_of((sender & 1) * size, LANE), size)
        input_out[lines, lanes] = arrived_ref[:, :size]
    for copy in copies:
        copy.wait()
    tops = jnp.zeros((1, LANE), jnp.float32)
    for distance, arrived_ref in enumerate(arrived_refs):
        sender = token ^ distance
        lines = pl.ds(pl.multiple_of(sender * cap, cap), cap)
        for side in range(2):
            lanes = slice(side * half, (side + 1) * half)
            gate = gate_ref[lines, lanes].astype(jnp.float32)
            sigmoid_value = 1.0 / (1.0 + jnp.exp(-gate))
            slope = sigmoid_value * (1.0 + gate * (1.0 - sigmoid_value))
            value = arrived_ref[side * cap : (side + 1) * cap, size : size + half].astype(jnp.float32)
            hidden = hidden_ref[lines, lanes].astype(jnp.float32)
            gate_out[lines, lanes] = (hidden * value * slope).astype(jnp.bfloat16)
        kinds = arrived_ref[:META, size + half :].astype(jnp.float32)
        tops = jnp.maximum(tops, kinds[0:1] + kinds[1:2] + kinds[2:3])
    lanes = lax.broadcasted_iota(jnp.int32, (1, LANE), 1)
    first = lax.broadcasted_iota(jnp.int32, scale_out.shape, 0)
    second = lax.broadcasted_iota(jnp.int32, scale_out.shape, 1)
    scales = jnp.zeros(scale_out.shape, jnp.float32)
    for j in range(delta_ref.shape[1]):
        for k in range(K):
            top = jnp.max(jnp.where(lanes == j * K + k, tops, 0.0))
            scales = jnp.where((first == j) & (second == k), top, scales)
            codes_out[:, j, k, :] = (delta_ref[:, j, k, :] / (top + scale_eps)).astype(jnp.bfloat16)
    scale_out[...] = scales


def paired(
    peer_count, rollout, lengths, route, up_codes, up_scales, block_rows, delta, adam_m, adam_v, gate_pre, hidden_grad
):
    send_rows, row_width = rollout.shape
    cap = 2 * send_rows // peer_count
    chips = peer_count // 2
    owned = BLK // peer_count
    own_rows, width = up_codes.shape
    mates = [(t, t ^ 1) for t in range(peer_count)]
    scales = up_scales.T
    spots = block_rows.size

    def hop(codes, turned):
        return lax.ppermute(codes, "tok", [(t, t ^ (4 if (t & 1) ^ turned else 2)) for t in range(peer_count)])

    codes_near = hop(up_codes, 0)
    codes_side = hop(up_codes, 1)
    mate_x = lax.ppermute(rollout, "tok", mates)
    first_out = call(
        learner_kernel,
        jax.ShapeDtypeStruct((peer_count, cap + owned, width), jnp.bfloat16),
        in_specs=[HBM] * 3,
        out_specs=VMEM,
        scratch_shapes=[
            pltpu.VMEM(gate_pre.shape, jnp.bfloat16),
            pltpu.VMEM(hidden_grad.shape, jnp.bfloat16),
            pltpu.VMEM(delta.shape, jnp.float32),
            pltpu.SemaphoreType.DMA((3,)),
        ],
    )(gate_pre, hidden_grad, delta)
    arrived = lax.all_to_all(first_out, "tok", split_axis=0, concat_axis=0, tiled=True)
    own_up = call(
        sender_kernel,
        jax.ShapeDtypeStruct((send_rows + META + BLK, width), jnp.bfloat16),
        in_specs=[SMEM, VMEM, HBM],
        out_specs=VMEM,
        scratch_shapes=[
            pltpu.VMEM((peer_count, cap, width), jnp.bfloat16),
            pltpu.VMEM((peer_count, owned, width), jnp.bfloat16),
            pltpu.SemaphoreType.DMA((2,)),
        ],
    )(lengths, route.reshape(1, send_rows), arrived)
    mate_up = lax.ppermute(own_up, "tok", mates)

    codes_far = hop(codes_near, 1)
    shared = (scales, block_rows, own_up, mate_up)
    early_sum, *backs = products((0, 1, 2), *shared, [up_codes, codes_near, codes_side], rollout, mate_x)
    weight_far, *backs = products((3,), *shared, [codes_far], *backs)
    parts = [backs[0]]
    for shift in range(1, chips):
        parts.append(lax.ppermute(backs[shift], "col", [(z, z ^ shift) for z in range(chips)]))
    own_sum, mate_sum = call(
        forward_kernel,
        [jax.ShapeDtypeStruct((send_rows, width), jnp.float32)] * 2,
        in_specs=[HBM] * 4,
        out_specs=[VMEM] * 2,
        scratch_shapes=[
            pltpu.VMEM((2 * send_rows, own_rows), jnp.bfloat16),
            pltpu.VMEM((own_rows, width), jnp.bfloat16),
            pltpu.VMEM((2 * send_rows, width), jnp.float32),
            pltpu.SemaphoreType.DMA((4,)),
        ],
    )(rollout, mate_x, weight_far, early_sum)
    other_sum = lax.ppermute(mate_sum, "tok", mates)

    gradient_parts = call(
        gradient_kernel,
        [jax.ShapeDtypeStruct((spots, owned, BLK), jnp.bfloat16)] * chips,
        in_specs=[SMEM] + [HBM] * 4,
        out_specs=[VMEM] * chips,
        scratch_shapes=[
            pltpu.VMEM((chips, spots, owned, BLK), jnp.bfloat16),
            pltpu.VMEM((spots, 2 * send_rows, BLK), jnp.bfloat16),
            pltpu.VMEM((2 * send_rows, width), jnp.bfloat16),
            pltpu.SemaphoreType.DMA((2 * spots + 2,)),
        ],
    )(block_rows, rollout, mate_x, own_up, mate_up)
    gradient_arrived = [gradient_parts[0]] + [
        lax.ppermute(gradient_parts[step], "tok", [(t, t ^ (2 * step)) for t in range(peer_count)])
        for step in range(1, chips)
    ]
    moment = jax.ShapeDtypeStruct(delta.shape, jnp.float32)
    new_delta, new_m, new_v, tops = call(
        adam_kernel,
        (moment, moment, moment, jax.ShapeDtypeStruct((META, LANE), jnp.bfloat16)),
        in_specs=[HBM] * (3 + chips),
        out_specs=(VMEM,) * 4,
        scratch_shapes=[pltpu.VMEM(delta.shape, jnp.float32)] * 3
        + [pltpu.VMEM((chips, spots, owned, BLK), jnp.bfloat16), pltpu.SemaphoreType.DMA((3 + chips,))],
    )(delta, adam_m, adam_v, *gradient_arrived)

    up_slots = call(
        spread_up_kernel,
        jax.ShapeDtypeStruct((peer_count, 2 * cap, width // 2 + LANE), jnp.bfloat16),
        in_specs=[VMEM] * 4,
        out_specs=VMEM,
    )(own_up, own_sum, other_sum, tops)
    spread_width = own_rows + width // 2 + LANE
    slots = call(
        spread_kernel,
        [jax.ShapeDtypeStruct((2 * cap, spread_width), jnp.bfloat16)] * peer_count,
        in_specs=[HBM] * (3 + len(parts)),
        out_specs=[VMEM] * peer_count,
        scratch_shapes=[
            pltpu.VMEM((peer_count, 2 * cap, own_rows), jnp.bfloat16),
            pltpu.VMEM((2, META, send_rows), jnp.bfloat16),
            pltpu.VMEM((len(parts), 2 * send_rows, own_rows), jnp.bfloat16),
            pltpu.SemaphoreType.DMA((2 + len(parts) + peer_count,)),
        ],
    )(own_up, mate_up, up_slots, *parts)
    sent = [slots[0]] + [
        lax.ppermute(slots[distance], "tok", [(t, t ^ distance) for t in range(peer_count)])
        for distance in range(1, peer_count)
    ]
    input_grad, gate_grad, delta_scale, delta_codes = call(
        finish_kernel,
        (
            jax.ShapeDtypeStruct((peer_count * cap, 2 * own_rows), jnp.bfloat16),
            jax.ShapeDtypeStruct(gate_pre.shape, jnp.bfloat16),
            jax.ShapeDtypeStruct(block_rows.shape, jnp.float32),
            jax.ShapeDtypeStruct(delta.shape, jnp.bfloat16),
        ),
        in_specs=[HBM] * 3 + [VMEM] * peer_count,
        out_specs=(VMEM,) * 4,
        scratch_shapes=[
            pltpu.VMEM(gate_pre.shape, jnp.bfloat16),
            pltpu.VMEM(hidden_grad.shape, jnp.bfloat16),
            pltpu.VMEM(delta.shape, jnp.float32),
            pltpu.SemaphoreType.DMA((3,)),
        ],
    )(gate_pre, hidden_grad, new_delta, *sent)
    return (input_grad, gate_grad, new_delta, new_m, new_v, delta_scale, delta_codes)


def per_device(tok_size, col_size, *arrays):
    rollout, up_codes = arrays[0], arrays[3]
    fits = (
        tok_size == 8 and col_size == 4
        and rollout.shape[0] == LANE
        and up_codes.shape[0] % LANE == 0
        and up_codes.shape[1] % BLK == 0
    )
    if fits:
        return paired(tok_size, *arrays)
    return any_mesh(*arrays)


def solution(mesh):
    placed = (
        P("tok", None),
        P("tok"),
        P("tok", None),
        P("tok", "col"),
        P(None, "col"),
        P("col", None),
        P("tok", "col", None, None),
        P("tok", "col", None, None),
        P("tok", "col", None, None),
        P("tok", "col"),
        P("tok", "col"),
    )
    return jax.shard_map(
        functools.partial(per_device, mesh.shape["tok"], mesh.shape["col"]),
        mesh=mesh,
        in_specs=placed,
        out_specs=(
            P("tok", "col"),
            P("tok", "col"),
            P("tok", "col", None, None),
            P("tok", "col", None, None),
            P("tok", "col", None, None),
            P("col", None),
            P("tok", "col", None, None),
        ),
        check_vma=False,
    )
```

```python
import functools

import jax
import jax.numpy as jnp
from jax import lax
from jax.experimental import pallas as pl
from jax.experimental.pallas import tpu as pltpu
from jax.sharding import PartitionSpec as P

BLK = 256
K = 2
RESP = 64
STEP = 1000


beta_first = 0.9
beta_second = 0.999
step_rate = 0.01
adam_eps = 1e-08
scale_eps = 1e-06


def silu_slope(operand):
    sigmoid_value = jax.nn.sigmoid(operand)
    return sigmoid_value * (1.0 + operand * (1.0 - sigmoid_value))


def dequant(code_rows, scales):
    row_count = code_rows.shape[0]
    block_count = scales.shape[0]
    width_blocks = scales.shape[1]
    block_of_row = jnp.arange(row_count, dtype=jnp.int32) // BLK
    selector = (block_of_row[:, None] == jnp.arange(block_count, dtype=jnp.int32)[None, :]).astype(
        jnp.float32
    )
    row_scales = jnp.dot(selector, scales, precision=lax.Precision.HIGHEST)
    spread = (
        code_rows.astype(jnp.float32).reshape(row_count, width_blocks, -1) * row_scales[:, :, None]
    )
    return spread.reshape(row_count, -1).astype(jnp.bfloat16)


def any_mesh(
    rollout,
    lengths,
    route,
    up_codes,
    up_scales,
    block_rows,
    delta,
    adam_m,
    adam_v,
    gate_pre,
    hidden_grad,
):
    peer_count = lax.axis_size("tok")
    send_rows = rollout.shape[0]
    row_width = rollout.shape[1]
    capacity = 2 * send_rows // peer_count
    row_ids = jnp.arange(send_rows, dtype=jnp.int32)
    seq_len = jnp.repeat(lengths, RESP)
    position = row_ids % RESP
    row_weight = jnp.where(position < seq_len, RESP / seq_len.astype(jnp.float32), 0.0)
    destination = route[:, 0]
    onehot = (destination[:, None] == jnp.arange(peer_count, dtype=jnp.int32)[None, :]).astype(
        jnp.int32
    )
    slot_index = jnp.sum((jnp.cumsum(onehot, axis=0) - 1) * onehot, axis=1)
    target = destination * capacity + slot_index
    weight_slots = (
        jnp.zeros((peer_count * capacity,), jnp.float32)
        .at[target]
        .set(row_weight)
        .reshape(peer_count, capacity)
    )
    buffer = (
        jnp.zeros((peer_count * capacity, row_width), jnp.bfloat16)
        .at[target]
        .set(rollout)
        .reshape(peer_count, capacity, row_width)
    )
    arrived, arrived_weight = (
        lax.all_to_all(buffer, "tok", split_axis=0, concat_axis=0, tiled=True),
        lax.all_to_all(
            weight_slots.astype(jnp.bfloat16), "tok", split_axis=0, concat_axis=0, tiled=True
        ).astype(weight_slots.dtype),
    )
    learn_x = arrived.reshape(peer_count * capacity, row_width)
    learn_w = arrived_weight.reshape(peer_count * capacity)
    rows_learn = learn_x.shape[0]
    column_count = up_codes.shape[1]
    blocks_here = column_count // BLK
    block_total = up_scales.shape[0]
    delta_full = lax.all_gather(delta.astype(jnp.bfloat16), "tok", axis=0, tiled=True)
    chosen = jnp.take(
        learn_x.reshape(rows_learn, block_total, BLK), block_rows.reshape(-1), axis=1
    ).reshape(rows_learn, blocks_here, K, BLK)
    activation = jax.nn.silu(gate_pre.astype(jnp.float32))
    up_grad = (hidden_grad.astype(jnp.float32) * activation * learn_w[:, None]).astype(jnp.bfloat16)
    up_grad_blocks = up_grad.reshape(rows_learn, blocks_here, BLK)
    delta_up = jnp.einsum(
        "rjkb,bjkc->rjc", chosen, delta_full, preferred_element_type=jnp.float32
    ).reshape(rows_learn, column_count)
    delta_back = jnp.einsum(
        "rjc,bjkc->rjkb", up_grad_blocks, delta_full, preferred_element_type=jnp.float32
    )
    selector = (
        block_rows.reshape(-1)[:, None] == jnp.arange(block_total, dtype=jnp.int32)[None, :]
    ).astype(jnp.float32)
    delta_input = jnp.einsum(
        "rqb,qd->rdb",
        delta_back.reshape(rows_learn, -1, BLK),
        selector,
        precision=lax.Precision.HIGHEST,
    ).reshape(rows_learn, row_width)
    weight = dequant(lax.all_gather(up_codes, "tok", axis=0, tiled=True), up_scales)
    base_up = jnp.dot(learn_x, weight, preferred_element_type=jnp.float32)
    weight = dequant(lax.all_gather(up_codes, "tok", axis=0, tiled=True), up_scales)
    base_input = lax.dot_general(
        up_grad, weight, (((1,), (1,)), ((), ())), preferred_element_type=jnp.float32
    )
    up_value = base_up + delta_up
    gate_grad = (
        hidden_grad.astype(jnp.float32)
        * up_value
        * silu_slope(gate_pre.astype(jnp.float32))
        * learn_w[:, None]
    ).astype(jnp.bfloat16)
    input_grad = lax.psum_scatter(
        base_input + delta_input, "col", scatter_dimension=1, tiled=True
    ).astype(jnp.bfloat16)
    owned_rows = BLK // peer_count
    summed_grad = lax.psum(
        jnp.einsum("rjkb,rjc->bjkc", chosen, up_grad_blocks, preferred_element_type=jnp.float32),
        "tok",
    )
    gradient = lax.dynamic_slice_in_dim(
        summed_grad, lax.axis_index("tok") * owned_rows, owned_rows, 0
    )
    new_m = beta_first * adam_m + (1.0 - beta_first) * gradient
    new_v = beta_second * adam_v + (1.0 - beta_second) * gradient * gradient
    corrected_m = new_m / (1.0 - beta_first**STEP)
    corrected_v = new_v / (1.0 - beta_second**STEP)
    new_delta = delta - step_rate * corrected_m / (jnp.sqrt(corrected_v) + adam_eps)
    local_max = jnp.max(jnp.abs(new_delta), axis=(0, 3))
    block_scale = lax.pmax(local_max, "tok")
    new_codes = (new_delta / (block_scale + scale_eps)[None, :, :, None]).astype(jnp.bfloat16)
    return (input_grad, gate_grad, new_delta, new_m, new_v, block_scale, new_codes)


LANE = 128
META = 16
FAST_LIMIT = 64 * 1024 * 1024


def call(kernel, out_shape, flops=0, moved=0, **extra):
    return pl.pallas_call(
        kernel,
        out_shape=out_shape,
        compiler_params=pltpu.CompilerParams(vmem_limit_bytes=FAST_LIMIT),
        cost_estimate=pl.CostEstimate(flops=flops, bytes_accessed=moved, transcendentals=0),
        **extra,
    )


VMEM = pl.BlockSpec(memory_space=pltpu.VMEM)
SMEM = pl.BlockSpec(memory_space=pltpu.SMEM)
HBM = pl.BlockSpec(memory_space=pltpu.HBM)
AFTER = pl.BlockSpec(memory_space=pl.ANY)


def own_place():
    token = lax.axis_index("tok")
    return token & 1, lax.shift_right_logical(token, 1)


def fetch(pairs, sems):
    copies = [pltpu.make_async_copy(*pair, sems.at[n]) for n, pair in enumerate(pairs)]
    for copy in copies:
        copy.start()
    return copies


def learner_kernel(gate_hbm, hidden_hbm, delta_hbm, out_ref, gate_ref, hidden_ref, delta_ref, sems):
    copies = fetch([(gate_hbm, gate_ref), (hidden_hbm, hidden_ref), (delta_hbm, delta_ref)], sems)
    peers, _, width = out_ref.shape
    cap = gate_ref.shape[0] // peers
    owned = delta_ref.shape[0]
    copies[0].wait()
    copies[1].wait()
    gate = gate_ref[...].astype(jnp.float32)
    raw = hidden_ref[...].astype(jnp.float32) * gate / (1.0 + jnp.exp(-gate))
    out_ref[:, :cap, :] = raw.astype(jnp.bfloat16).reshape(peers, cap, width)
    copies[2].wait()
    for j in range(delta_ref.shape[1]):
        for k in range(K):
            half = delta_ref[:, j, k, :].astype(jnp.bfloat16)
            for peer in range(k, peers, K):
                out_ref[peer, cap:, j * BLK : (j + 1) * BLK] = half


def place_matrix(target_row, slots):
    rows = target_row.shape[1]
    ids = lax.broadcasted_iota(jnp.int32, (slots, rows), 0)
    return (ids == target_row).astype(jnp.bfloat16)


def as_column(row):
    size = row.shape[1]
    first = lax.broadcasted_iota(jnp.int32, (size, size), 0)
    second = lax.broadcasted_iota(jnp.int32, (size, size), 1)
    return jnp.sum(jnp.where(first == second, row, 0.0), axis=1, keepdims=True)


def weight_of(length_row):
    position = lax.rem(lax.broadcasted_iota(jnp.int32, length_row.shape, 1), RESP)
    return jnp.where(position.astype(jnp.float32) < length_row, RESP / length_row, 0.0)


def sender_kernel(lengths_ref, route_ref, arrived_hbm, out_ref, raw_ref, delta_ref, sems):
    peers, cap, width = raw_ref.shape
    rows = route_ref.shape[1]
    copies = fetch([(arrived_hbm.at[:, :cap, :], raw_ref), (arrived_hbm.at[:, cap:, :], delta_ref)], sems)
    route = route_ref[...]
    named = (lax.broadcasted_iota(jnp.int32, (max(peers, 16), rows), 0) == route).astype(jnp.float32)
    before = (
        lax.broadcasted_iota(jnp.int32, (rows, rows), 0)
        < lax.broadcasted_iota(jnp.int32, (rows, rows), 1)
    ).astype(jnp.bfloat16)
    ranks = jnp.dot(named.astype(jnp.bfloat16), before, preferred_element_type=jnp.float32)
    slot = jnp.sum(named * ranks, axis=0, keepdims=True).astype(jnp.int32)
    target = route * cap + slot
    row_ids = lax.broadcasted_iota(jnp.int32, (1, rows), 1)
    length_row = jnp.zeros((1, rows), jnp.float32)
    for seq in range(rows // RESP):
        mine = (row_ids >= seq * RESP) & (row_ids < (seq + 1) * RESP)
        length_row = jnp.where(mine, lengths_ref[seq].astype(jnp.float32), length_row)
    place = place_matrix(target, peers * cap)
    copies[0].wait()
    raw = raw_ref[...].reshape(peers * cap, width)
    picked = lax.dot_general(
        place, raw, (((0,), (0,)), ((), ())), preferred_element_type=jnp.float32
    )
    out_ref[:rows, :] = (picked * as_column(weight_of(length_row))).astype(jnp.bfloat16)
    out_ref[rows : rows + META, :] = jnp.zeros((META, width), jnp.bfloat16)
    meta_ids = lax.broadcasted_iota(jnp.int32, (META, rows), 0)
    meta = jnp.where(meta_ids == 0, target.astype(jnp.float32), 0.0)
    meta = jnp.where(meta_ids == 1, length_row, meta)
    out_ref[rows : rows + META, :rows] = meta.astype(jnp.bfloat16)
    copies[1].wait()
    out_ref[rows + META :, :] = delta_ref[...].reshape(-1, width)


def gradient_kernel(rows_ref, own_x, mate_x, own_up, mate_up, *refs):
    out_refs, (held_ref, x_ref, up_ref, sems) = refs[:-4], refs[-4:]
    chips, spots, owned, width = held_ref.shape
    rows = own_x.shape[0]
    pairs = []
    for seat, (x_hbm, up_hbm) in enumerate(((own_x, own_up), (mate_x, mate_up))):
        lines = slice(seat * rows, (seat + 1) * rows)
        pairs.append((up_hbm.at[:rows, :], up_ref.at[lines]))
        for spot in range(spots):
            lanes = pl.ds(pl.multiple_of(rows_ref[spot // K, spot % K] * BLK, BLK), BLK)
            pairs.append((x_hbm.at[:, lanes], x_ref.at[spot, lines]))
    for copy in fetch(pairs, sems):
        copy.wait()
    core, own_chip = own_place()
    for spot in range(spots):
        j = spot // K
        full = lax.dot_general(
            x_ref[spot],
            up_ref[:, j * BLK : (j + 1) * BLK],
            (((0,), (0,)), ((), ())),
            preferred_element_type=jnp.float32,
        ).reshape(chips, 2, owned, width)
        held_ref[:, spot] = jnp.where(core == 0, full[:, 0], full[:, 1]).astype(jnp.bfloat16)
    for distance, out_ref in enumerate(out_refs):
        out_ref[...] = held_ref[own_chip ^ distance]


def adam_kernel(delta_hbm, m_hbm, v_hbm, *refs):
    delta_out, m_out, v_out, max_out, delta_ref, m_ref, v_ref, grad_ref, sems = refs[-9:]
    chips = grad_ref.shape[0]
    pairs = [(delta_hbm, delta_ref), (m_hbm, m_ref), (v_hbm, v_ref)]
    for copy in fetch(pairs + [(refs[chip], grad_ref.at[chip]) for chip in range(chips)], sems):
        copy.wait()
    ids = lax.broadcasted_iota(jnp.int32, max_out.shape, 1)
    tops = jnp.zeros(max_out.shape, jnp.float32)
    for j in range(delta_ref.shape[1]):
        for k in range(K):
            spot = j * K + k
            gradient = grad_ref[0, spot].astype(jnp.float32)
            for chip in range(1, chips):
                gradient = gradient + grad_ref[chip, spot].astype(jnp.float32)
            new_m = beta_first * m_ref[:, j, k, :] + (1.0 - beta_first) * gradient
            new_v = beta_second * v_ref[:, j, k, :] + (1.0 - beta_second) * gradient * gradient
            corrected_m = new_m / (1.0 - beta_first**STEP)
            corrected_v = new_v / (1.0 - beta_second**STEP)
            new_delta = delta_ref[:, j, k, :] - step_rate * corrected_m / (
                jnp.sqrt(corrected_v) + adam_eps
            )
            m_out[:, j, k, :] = new_m
            v_out[:, j, k, :] = new_v
            delta_out[:, j, k, :] = new_delta
            tops = jnp.where(ids == spot, jnp.max(jnp.abs(new_delta)), tops)
    high = tops.astype(jnp.bfloat16).astype(jnp.float32)
    middle = (tops - high).astype(jnp.bfloat16).astype(jnp.float32)
    low = tops - high - middle
    kinds = lax.broadcasted_iota(jnp.int32, max_out.shape, 0)
    tops = jnp.where(kinds == 0, high, jnp.where(kinds == 1, middle, low))
    max_out[...] = jnp.where(kinds < 3, tops, 0.0).astype(jnp.bfloat16)


def block_order(core, step):
    return (0, 1 + core, 2 - core, 3)[step]


def scaled(codes_ref, scales_ref, block, spot, lines, lanes):
    return (codes_ref[spot, lines, lanes].astype(jnp.float32) * scales_ref[lanes.start // BLK, block]).astype(
        jnp.bfloat16
    )


def product_kernel(
    scales_ref, rows_ref, own_up, mate_up, own_x, mate_x, *refs
):
    codes_hbm, (sum_ref, *back_refs), (codes, weight, up, delta, x, sems) = refs[:3], refs[3:8], refs[8:]
    rows = own_x.shape[0]
    core, own_chip = own_place()
    turn = own_chip ^ lax.axis_index("col")
    size, width = weight.shape[1:]
    tiles = size // LANE
    pairs = row_pairs(own_up, mate_up, up, delta, core)
    shared = len(pairs)
    starts = []
    for step in range(3):
        first_tile = (2 * (own_chip ^ block_order(core, step)) + core) * tiles
        starts.append(first_tile)
        lanes = pl.ds(pl.multiple_of(first_tile * LANE, LANE), size)
        pairs.append((codes_hbm[step], codes.at[step]))
        pairs.append((own_x.at[:, lanes], x.at[step, :rows]))
        pairs.append((mate_x.at[:, lanes], x.at[step, rows:]))
    copies = fetch(pairs, sems)
    for step in range(3):
        for copy in copies[shared + 3 * step : shared + 3 * (step + 1)]:
            copy.wait()
        for tile in range(tiles):
            block = lax.div(starts[step] + tile, BLK // LANE)
            lines = slice(tile * LANE, (tile + 1) * LANE)
            for j in range(width // BLK):
                lanes = slice(j * BLK, (j + 1) * BLK)
                weight[step, lines, lanes] = scaled(codes, scales_ref, block, step, lines, lanes)
        if step == 0:
            for copy in copies[:shared]:
                copy.wait()
        for j in range(width // BLK):
            lanes = slice(j * BLK, (j + 1) * BLK)
            for k in range(K):
                for piece in range(BLK // LANE):
                    tile = rows_ref[j, k] * (BLK // LANE) + piece - starts[step]

                    @pl.when((tile >= 0) & (tile < tiles))
                    def _():
                        lines = pl.ds(pl.multiple_of(tile * LANE, LANE), LANE)
                        extra = delta[k, piece * LANE : (piece + 1) * LANE, lanes].astype(jnp.float32)
                        held = weight[step, lines, lanes].astype(jnp.float32)
                        weight[step, lines, lanes] = (held + extra).astype(jnp.bfloat16)

        back = lax.dot_general(
            up[...], weight[step], (((1,), (1,)), ((), ())), preferred_element_type=jnp.float32
        ).astype(jnp.bfloat16)
        for shift, back_ref in enumerate(back_refs):

            @pl.when((turn ^ block_order(core, step)) == shift)
            def _():
                back_ref[...] = back

        part_sum = jnp.dot(x[step], weight[step], preferred_element_type=jnp.float32)
        if step == 0:
            sum_ref[...] = part_sum
        else:
            sum_ref[...] += part_sum


def row_pairs(own_up, mate_up, up, delta, core):
    rows = up.shape[0] // 2
    pairs = []
    for seat, up_hbm in enumerate((own_up, mate_up)):
        pairs.append((up_hbm.at[:rows, :], up.at[seat * rows : (seat + 1) * rows]))
        pairs.append((up_hbm.at[rows + META :, :], delta.at[core ^ seat]))
    return pairs


def far_kernel(scales_ref, rows_ref, own_up, mate_up, codes_hbm, *refs):
    weight_out, *back_refs = refs[4:9]
    codes, weight, up, delta, back, sems, out_sems = refs[9:]
    core, own_chip = own_place()
    turn = own_chip ^ lax.axis_index("col")
    size, width = weight.shape
    tiles = size // LANE
    first_tile = (2 * (own_chip ^ 3) + core) * tiles
    copies = fetch([(codes_hbm, codes.at[0])] + row_pairs(own_up, mate_up, up, delta, core), sems)
    copies[0].wait()
    for tile in range(tiles):
        block = lax.div(first_tile + tile, BLK // LANE)
        lines = slice(tile * LANE, (tile + 1) * LANE)
        for j in range(width // BLK):
            lanes = slice(j * BLK, (j + 1) * BLK)
            weight[lines, lanes] = scaled(codes, scales_ref, block, 0, lines, lanes)
    for copy in copies[1:]:
        copy.wait()
    for j in range(width // BLK):
        lanes = slice(j * BLK, (j + 1) * BLK)
        for k in range(K):
            for piece in range(BLK // LANE):
                tile = rows_ref[j, k] * (BLK // LANE) + piece - first_tile

                @pl.when((tile >= 0) & (tile < tiles))
                def _():
                    lines = pl.ds(pl.multiple_of(tile * LANE, LANE), LANE)
                    extra = delta[k, piece * LANE : (piece + 1) * LANE, lanes].astype(jnp.float32)
                    held = weight[lines, lanes].astype(jnp.float32)
                    weight[lines, lanes] = (held + extra).astype(jnp.bfloat16)

    weight_copy = pltpu.make_async_copy(weight, weight_out, out_sems.at[1])
    weight_copy.start()
    back[...] = lax.dot_general(
        up[...], weight[...], (((1,), (1,)), ((), ())), preferred_element_type=jnp.float32
    ).astype(jnp.bfloat16)
    for shift, back_ref in enumerate(back_refs):

        @pl.when((turn ^ 3) == shift)
        def _():
            back_copy = pltpu.make_async_copy(back, back_ref, out_sems.at[0])
            back_copy.start()
            back_copy.wait()

    weight_copy.wait()


def forward_kernel(own_x, mate_x, weight_hbm, sum_hbm, own_out, mate_out, x, weight, total, sems):
    size = weight.shape[0]
    rows = own_out.shape[0]
    core, own_chip = own_place()
    lanes = pl.ds(pl.multiple_of((2 * (own_chip ^ 3) + core) * size, LANE), size)
    pairs = [(own_x.at[:, lanes], x.at[:rows]), (mate_x.at[:, lanes], x.at[rows:])]
    for copy in fetch(pairs + [(weight_hbm, weight), (sum_hbm, total)], sems):
        copy.wait()
    full = total[...] + jnp.dot(x[...], weight[...], preferred_element_type=jnp.float32)
    own_out[...] = full[:rows]
    mate_out[...] = full[rows:]


def spread_up_kernel(own_up, own_sum, other_sum, tops_ref, out_ref):
    peers, lines, _ = out_ref.shape
    rows, width = own_sum.shape
    cap, half = lines // 2, width // 2
    target = own_up[rows : rows + META, :rows].astype(jnp.float32)
    place = place_matrix(target[0:1].astype(jnp.int32), peers * cap)
    value = (own_sum[...] + other_sum[...]) * as_column(weight_of(target[1:2]))
    placed = jnp.dot(place, value.astype(jnp.bfloat16), preferred_element_type=jnp.float32)
    placed = placed.astype(jnp.bfloat16).reshape(peers, cap, width)
    for side in range(2):
        out_ref[:, side * cap : (side + 1) * cap, :half] = placed[:, :, side * half : (side + 1) * half]
    for peer in range(peers):
        out_ref[peer, :META, half:] = tops_ref[...]
        out_ref[peer, META:, half:] = jnp.zeros((lines - META, LANE), jnp.bfloat16)


def spread_kernel(own_up, mate_up, up_slots, *refs):
    parts_hbm, out_refs = refs[:4], refs[4:-5]
    held_ref, meta_ref, parts_ref, sems, out_sems = refs[-5:]
    _, rows, size = parts_ref.shape
    rows = rows // 2
    peers = held_ref.shape[0]
    cap = 2 * rows // peers
    core, _ = own_place()
    token = lax.axis_index("tok")
    pairs = [(up.at[rows : rows + META, :rows], meta_ref.at[seat]) for seat, up in enumerate((own_up, mate_up))]
    pairs += [(part, parts_ref.at[n]) for n, part in enumerate(parts_hbm)]
    pairs.append((up_slots, held_ref.at[:, :, size:]))
    copies = fetch(pairs, sems)
    for copy in copies[:-1]:
        copy.wait()
    for seat in range(2):
        lines = slice(seat * rows, (seat + 1) * rows)
        summed = parts_ref[0, lines].astype(jnp.float32)
        for part in range(1, len(parts_hbm)):
            summed = summed + parts_ref[part, lines].astype(jnp.float32)
        target = meta_ref[seat].astype(jnp.float32)
        place = place_matrix(target[0:1].astype(jnp.int32), peers * cap)
        placed = jnp.dot(place, summed.astype(jnp.bfloat16), preferred_element_type=jnp.float32)
        start = pl.multiple_of((core ^ seat) * cap, cap)
        held_ref[:, pl.ds(start, cap), :size] = placed.astype(jnp.bfloat16).reshape(peers, cap, size)
    copies[-1].wait()
    out_copies = fetch([(held_ref.at[token ^ d], far_ref) for d, far_ref in enumerate(out_refs)], out_sems)
    for copy in out_copies:
        copy.wait()


def finish_kernel(gate_hbm, hidden_hbm, delta_hbm, *refs, order):
    arrived_hbm = refs[:-10]
    input_out, gate_out, scale_out, codes_out, gate_ref, hidden_ref, delta_ref, held_ref, sems, out_sems = refs[-10:]
    size = input_out.shape[1] // 2
    peers = len(arrived_hbm)
    cap = gate_ref.shape[0] // peers
    half = gate_ref.shape[1] // 2
    token = lax.axis_index("tok")
    pairs = [(gate_hbm, gate_ref), (hidden_hbm, hidden_ref), (delta_hbm, delta_ref)]
    pairs += [(ref, held_ref.at[number]) for number, ref in enumerate(arrived_hbm)]
    copies = fetch(pairs, sems)
    out_copies = []
    for number, distance in enumerate(order):
        sender = token ^ distance
        lines = pl.ds(pl.multiple_of((sender >> 1) * 2 * cap, 2 * cap), 2 * cap)
        lanes = pl.ds(pl.multiple_of((sender & 1) * size, LANE), size)
        copies[3 + number].wait()
        out_copies.append(
            pltpu.make_async_copy(
                held_ref.at[number, :, :size], input_out.at[lines, lanes], out_sems.at[number]
            )
        )
        out_copies[-1].start()
    for copy in copies[:3]:
        copy.wait()
    tops = jnp.zeros((1, LANE), jnp.float32)
    for number, distance in enumerate(order):
        lines = pl.ds(pl.multiple_of((token ^ distance) * cap, cap), cap)
        for side in range(2):
            lanes = slice(side * half, (side + 1) * half)
            gate = gate_ref[lines, lanes].astype(jnp.float32)
            sigmoid_value = 1.0 / (1.0 + jnp.exp(-gate))
            slope = sigmoid_value * (1.0 + gate * (1.0 - sigmoid_value))
            value = held_ref[number, side * cap : (side + 1) * cap, size : size + half].astype(jnp.float32)
            hidden = hidden_ref[lines, lanes].astype(jnp.float32)
            gate_out[lines, lanes] = (hidden * value * slope).astype(jnp.bfloat16)
        kinds = held_ref[number, :META, size + half :].astype(jnp.float32)
        tops = jnp.maximum(tops, kinds[0:1] + kinds[1:2] + kinds[2:3])
    lanes = lax.broadcasted_iota(jnp.int32, (1, LANE), 1)
    first = lax.broadcasted_iota(jnp.int32, scale_out.shape, 0)
    second = lax.broadcasted_iota(jnp.int32, scale_out.shape, 1)
    scales = jnp.zeros(scale_out.shape, jnp.float32)
    for j in range(delta_ref.shape[1]):
        for k in range(K):
            top = jnp.max(jnp.where(lanes == j * K + k, tops, 0.0))
            scales = jnp.where((first == j) & (second == k), top, scales)
            codes_out[:, j, k, :] = (delta_ref[:, j, k, :] / (top + scale_eps)).astype(jnp.bfloat16)
    scale_out[...] = scales
    for copy in out_copies:
        copy.wait()


def paired(
    peer_count, rollout, lengths, route, up_codes, up_scales, block_rows, delta, adam_m, adam_v, gate_pre, hidden_grad
):
    send_rows, row_width = rollout.shape
    cap = 2 * send_rows // peer_count
    chips = peer_count // 2
    owned = BLK // peer_count
    own_rows, width = up_codes.shape
    mates = [(t, t ^ 1) for t in range(peer_count)]
    scales = up_scales.T
    spots = block_rows.size

    def hop(codes, turned):
        return lax.ppermute(codes, "tok", [(t, t ^ (4 if (t & 1) ^ turned else 2)) for t in range(peer_count)])

    codes_near = hop(up_codes, 0)
    codes_side = hop(up_codes, 1)
    mate_x = lax.ppermute(rollout, "tok", mates)
    first_out = call(
        learner_kernel,
        jax.ShapeDtypeStruct((peer_count, cap + owned, width), jnp.bfloat16),
        in_specs=[HBM] * 3,
        out_specs=VMEM,
        scratch_shapes=[
            pltpu.VMEM(gate_pre.shape, jnp.bfloat16),
            pltpu.VMEM(hidden_grad.shape, jnp.bfloat16),
            pltpu.VMEM(delta.shape, jnp.float32),
            pltpu.SemaphoreType.DMA((3,)),
        ],
    )(gate_pre, hidden_grad, delta)
    arrived = lax.all_to_all(first_out, "tok", split_axis=0, concat_axis=0, tiled=True)
    own_up = call(
        sender_kernel,
        jax.ShapeDtypeStruct((send_rows + META + BLK, width), jnp.bfloat16),
        in_specs=[SMEM, VMEM, HBM],
        out_specs=VMEM,
        scratch_shapes=[
            pltpu.VMEM((peer_count, cap, width), jnp.bfloat16),
            pltpu.VMEM((peer_count, owned, width), jnp.bfloat16),
            pltpu.SemaphoreType.DMA((2,)),
        ],
    )(lengths, route.reshape(1, send_rows), arrived)
    mate_up = lax.ppermute(own_up, "tok", mates)

    codes_far = hop(codes_near, 1)
    back = jax.ShapeDtypeStruct((2 * send_rows, own_rows), jnp.bfloat16)
    row_scratch = [
        pltpu.VMEM((2 * send_rows, width), jnp.bfloat16),
        pltpu.VMEM((K, BLK, width), jnp.bfloat16),
    ]
    early_sum, *backs = call(
        product_kernel,
        [jax.ShapeDtypeStruct((2 * send_rows, width), jnp.float32)] + [back] * chips,
        in_specs=[SMEM] * 2 + [HBM] * 7,
        out_specs=[VMEM] * (1 + chips),
        scratch_shapes=[pltpu.VMEM((3, own_rows, width), jnp.bfloat16)] * 2
        + row_scratch
        + [pltpu.VMEM((3, 2 * send_rows, own_rows), jnp.bfloat16), pltpu.SemaphoreType.DMA((13,))],
    )(scales, block_rows, own_up, mate_up, rollout, mate_x, up_codes, codes_near, codes_side)
    weight_far, *backs = call(
        far_kernel,
        [jax.ShapeDtypeStruct((own_rows, width), jnp.bfloat16)] + [back] * chips,
        in_specs=[SMEM] * 2 + [HBM] * (3 + chips),
        out_specs=[HBM] * (1 + chips),
        scratch_shapes=[
            pltpu.VMEM((1, own_rows, width), jnp.bfloat16),
            pltpu.VMEM((own_rows, width), jnp.bfloat16),
        ]
        + row_scratch
        + [
            pltpu.VMEM(back.shape, jnp.bfloat16),
            pltpu.SemaphoreType.DMA((5,)),
            pltpu.SemaphoreType.DMA((2,)),
        ],
        input_output_aliases={5 + n: 1 + n for n in range(chips)},
    )(scales, block_rows, own_up, mate_up, codes_far, *backs)
    parts = [backs[0]]
    for shift in range(1, chips):
        parts.append(lax.ppermute(backs[shift], "col", [(z, z ^ shift) for z in range(chips)]))
    own_sum, mate_sum = call(
        forward_kernel,
        [jax.ShapeDtypeStruct((send_rows, width), jnp.float32)] * 2,
        in_specs=[HBM] * 4,
        out_specs=[VMEM] * 2,
        scratch_shapes=[
            pltpu.VMEM((2 * send_rows, own_rows), jnp.bfloat16),
            pltpu.VMEM((own_rows, width), jnp.bfloat16),
            pltpu.VMEM((2 * send_rows, width), jnp.float32),
            pltpu.SemaphoreType.DMA((4,)),
        ],
    )(rollout, mate_x, weight_far, early_sum)
    other_sum = lax.ppermute(mate_sum, "tok", mates)

    gradient_parts = call(
        gradient_kernel,
        [jax.ShapeDtypeStruct((spots, owned, BLK), jnp.bfloat16)] * chips,
        in_specs=[SMEM] + [HBM] * 4,
        out_specs=[VMEM] * chips,
        scratch_shapes=[
            pltpu.VMEM((chips, spots, owned, BLK), jnp.bfloat16),
            pltpu.VMEM((spots, 2 * send_rows, BLK), jnp.bfloat16),
            pltpu.VMEM((2 * send_rows, width), jnp.bfloat16),
            pltpu.SemaphoreType.DMA((2 * spots + 2,)),
        ],
    )(block_rows, rollout, mate_x, own_up, mate_up)
    gradient_arrived = [gradient_parts[0]] + [
        lax.ppermute(gradient_parts[step], "tok", [(t, t ^ (2 * step)) for t in range(peer_count)])
        for step in range(1, chips)
    ]
    moment = jax.ShapeDtypeStruct(delta.shape, jnp.float32)
    new_delta, new_m, new_v, tops = call(
        adam_kernel,
        (moment, moment, moment, jax.ShapeDtypeStruct((META, LANE), jnp.bfloat16)),
        in_specs=[HBM] * (3 + chips),
        out_specs=(VMEM,) * 4,
        scratch_shapes=[pltpu.VMEM(delta.shape, jnp.float32)] * 3
        + [pltpu.VMEM((chips, spots, owned, BLK), jnp.bfloat16), pltpu.SemaphoreType.DMA((3 + chips,))],
    )(delta, adam_m, adam_v, *gradient_arrived)

    up_slots = call(
        spread_up_kernel,
        jax.ShapeDtypeStruct((peer_count, 2 * cap, width // 2 + LANE), jnp.bfloat16),
        in_specs=[VMEM] * 4,
        out_specs=VMEM,
    )(own_up, own_sum, other_sum, tops)
    spread_width = own_rows + width // 2 + LANE
    slots = call(
        spread_kernel,
        [jax.ShapeDtypeStruct((2 * cap, spread_width), jnp.bfloat16)] * peer_count,
        in_specs=[HBM] * (3 + len(parts)),
        out_specs=[HBM] * peer_count,
        scratch_shapes=[
            pltpu.VMEM((peer_count, 2 * cap, spread_width), jnp.bfloat16),
            pltpu.VMEM((2, META, send_rows), jnp.bfloat16),
            pltpu.VMEM((len(parts), 2 * send_rows, own_rows), jnp.bfloat16),
            pltpu.SemaphoreType.DMA((3 + len(parts),)),
            pltpu.SemaphoreType.DMA((peer_count,)),
        ],
    )(own_up, mate_up, up_slots, *parts)
    sent = {}
    for distance in sorted(range(1, peer_count), key=lambda d: (-bin(d >> 1).count("1"), d)):
        sent[distance] = lax.ppermute(
            slots[distance], "tok", [(t, t ^ distance) for t in range(peer_count)]
        )
    sent[0] = slots[0]
    order = list(sent)
    input_grad, gate_grad, delta_scale, delta_codes = call(
        functools.partial(finish_kernel, order=order),
        (
            jax.ShapeDtypeStruct((peer_count * cap, 2 * own_rows), jnp.bfloat16),
            jax.ShapeDtypeStruct(gate_pre.shape, jnp.bfloat16),
            jax.ShapeDtypeStruct(block_rows.shape, jnp.float32),
            jax.ShapeDtypeStruct(delta.shape, jnp.bfloat16),
        ),
        in_specs=[HBM] * (3 + peer_count),
        out_specs=(HBM,) + (VMEM,) * 3,
        scratch_shapes=[
            pltpu.VMEM(gate_pre.shape, jnp.bfloat16),
            pltpu.VMEM(hidden_grad.shape, jnp.bfloat16),
            pltpu.VMEM(delta.shape, jnp.float32),
            pltpu.VMEM((peer_count, 2 * cap, spread_width), jnp.bfloat16),
            pltpu.SemaphoreType.DMA((3 + peer_count,)),
            pltpu.SemaphoreType.DMA((peer_count,)),
        ],
    )(gate_pre, hidden_grad, new_delta, *[sent[distance] for distance in order])
    return (input_grad, gate_grad, new_delta, new_m, new_v, delta_scale, delta_codes)


def per_device(tok_size, col_size, *arrays):
    rollout, up_codes = arrays[0], arrays[3]
    fits = (
        tok_size == 8 and col_size == 4
        and rollout.shape[0] == LANE
        and up_codes.shape[0] % LANE == 0
        and up_codes.shape[1] % BLK == 0
    )
    if fits:
        return paired(tok_size, *arrays)
    return any_mesh(*arrays)


def solution(mesh):
    placed = (
        P("tok", None),
        P("tok"),
        P("tok", None),
        P("tok", "col"),
        P(None, "col"),
        P("col", None),
        P("tok", "col", None, None),
        P("tok", "col", None, None),
        P("tok", "col", None, None),
        P("tok", "col"),
        P("tok", "col"),
    )
    return jax.shard_map(
        functools.partial(per_device, mesh.shape["tok"], mesh.shape["col"]),
        mesh=mesh,
        in_specs=placed,
        out_specs=(
            P("tok", "col"),
            P("tok", "col"),
            P("tok", "col", None, None),
            P("tok", "col", None, None),
            P("tok", "col", None, None),
            P("col", None),
            P("tok", "col", None, None),
        ),
        check_vma=False,
    )
```

```python
import functools

import jax
import jax.numpy as jnp
from jax import lax
from jax.experimental import pallas as pl
from jax.experimental.pallas import tpu as pltpu
from jax.sharding import PartitionSpec as P

BLK = 256
K = 2
RESP = 64
STEP = 1000


beta_first = 0.9
beta_second = 0.999
step_rate = 0.01
adam_eps = 1e-08
scale_eps = 1e-06


def silu_slope(operand):
    sigmoid_value = jax.nn.sigmoid(operand)
    return sigmoid_value * (1.0 + operand * (1.0 - sigmoid_value))


def dequant(code_rows, scales):
    row_count = code_rows.shape[0]
    block_count = scales.shape[0]
    width_blocks = scales.shape[1]
    block_of_row = jnp.arange(row_count, dtype=jnp.int32) // BLK
    selector = (block_of_row[:, None] == jnp.arange(block_count, dtype=jnp.int32)[None, :]).astype(
        jnp.float32
    )
    row_scales = jnp.dot(selector, scales, precision=lax.Precision.HIGHEST)
    spread = (
        code_rows.astype(jnp.float32).reshape(row_count, width_blocks, -1) * row_scales[:, :, None]
    )
    return spread.reshape(row_count, -1).astype(jnp.bfloat16)


def any_mesh(
    rollout,
    lengths,
    route,
    up_codes,
    up_scales,
    block_rows,
    delta,
    adam_m,
    adam_v,
    gate_pre,
    hidden_grad,
):
    peer_count = lax.axis_size("tok")
    send_rows = rollout.shape[0]
    row_width = rollout.shape[1]
    capacity = 2 * send_rows // peer_count
    row_ids = jnp.arange(send_rows, dtype=jnp.int32)
    seq_len = jnp.repeat(lengths, RESP)
    position = row_ids % RESP
    row_weight = jnp.where(position < seq_len, RESP / seq_len.astype(jnp.float32), 0.0)
    destination = route[:, 0]
    onehot = (destination[:, None] == jnp.arange(peer_count, dtype=jnp.int32)[None, :]).astype(
        jnp.int32
    )
    slot_index = jnp.sum((jnp.cumsum(onehot, axis=0) - 1) * onehot, axis=1)
    target = destination * capacity + slot_index
    weight_slots = (
        jnp.zeros((peer_count * capacity,), jnp.float32)
        .at[target]
        .set(row_weight)
        .reshape(peer_count, capacity)
    )
    buffer = (
        jnp.zeros((peer_count * capacity, row_width), jnp.bfloat16)
        .at[target]
        .set(rollout)
        .reshape(peer_count, capacity, row_width)
    )
    arrived, arrived_weight = (
        lax.all_to_all(buffer, "tok", split_axis=0, concat_axis=0, tiled=True),
        lax.all_to_all(
            weight_slots.astype(jnp.bfloat16), "tok", split_axis=0, concat_axis=0, tiled=True
        ).astype(weight_slots.dtype),
    )
    learn_x = arrived.reshape(peer_count * capacity, row_width)
    learn_w = arrived_weight.reshape(peer_count * capacity)
    rows_learn = learn_x.shape[0]
    column_count = up_codes.shape[1]
    blocks_here = column_count // BLK
    block_total = up_scales.shape[0]
    delta_full = lax.all_gather(delta.astype(jnp.bfloat16), "tok", axis=0, tiled=True)
    chosen = jnp.take(
        learn_x.reshape(rows_learn, block_total, BLK), block_rows.reshape(-1), axis=1
    ).reshape(rows_learn, blocks_here, K, BLK)
    activation = jax.nn.silu(gate_pre.astype(jnp.float32))
    up_grad = (hidden_grad.astype(jnp.float32) * activation * learn_w[:, None]).astype(jnp.bfloat16)
    up_grad_blocks = up_grad.reshape(rows_learn, blocks_here, BLK)
    delta_up = jnp.einsum(
        "rjkb,bjkc->rjc", chosen, delta_full, preferred_element_type=jnp.float32
    ).reshape(rows_learn, column_count)
    delta_back = jnp.einsum(
        "rjc,bjkc->rjkb", up_grad_blocks, delta_full, preferred_element_type=jnp.float32
    )
    selector = (
        block_rows.reshape(-1)[:, None] == jnp.arange(block_total, dtype=jnp.int32)[None, :]
    ).astype(jnp.float32)
    delta_input = jnp.einsum(
        "rqb,qd->rdb",
        delta_back.reshape(rows_learn, -1, BLK),
        selector,
        precision=lax.Precision.HIGHEST,
    ).reshape(rows_learn, row_width)
    weight = dequant(lax.all_gather(up_codes, "tok", axis=0, tiled=True), up_scales)
    base_up = jnp.dot(learn_x, weight, preferred_element_type=jnp.float32)
    weight = dequant(lax.all_gather(up_codes, "tok", axis=0, tiled=True), up_scales)
    base_input = lax.dot_general(
        up_grad, weight, (((1,), (1,)), ((), ())), preferred_element_type=jnp.float32
    )
    up_value = base_up + delta_up
    gate_grad = (
        hidden_grad.astype(jnp.float32)
        * up_value
        * silu_slope(gate_pre.astype(jnp.float32))
        * learn_w[:, None]
    ).astype(jnp.bfloat16)
    input_grad = lax.psum_scatter(
        base_input + delta_input, "col", scatter_dimension=1, tiled=True
    ).astype(jnp.bfloat16)
    owned_rows = BLK // peer_count
    summed_grad = lax.psum(
        jnp.einsum("rjkb,rjc->bjkc", chosen, up_grad_blocks, preferred_element_type=jnp.float32),
        "tok",
    )
    gradient = lax.dynamic_slice_in_dim(
        summed_grad, lax.axis_index("tok") * owned_rows, owned_rows, 0
    )
    new_m = beta_first * adam_m + (1.0 - beta_first) * gradient
    new_v = beta_second * adam_v + (1.0 - beta_second) * gradient * gradient
    corrected_m = new_m / (1.0 - beta_first**STEP)
    corrected_v = new_v / (1.0 - beta_second**STEP)
    new_delta = delta - step_rate * corrected_m / (jnp.sqrt(corrected_v) + adam_eps)
    local_max = jnp.max(jnp.abs(new_delta), axis=(0, 3))
    block_scale = lax.pmax(local_max, "tok")
    new_codes = (new_delta / (block_scale + scale_eps)[None, :, :, None]).astype(jnp.bfloat16)
    return (input_grad, gate_grad, new_delta, new_m, new_v, block_scale, new_codes)


LANE = 128
META = 16
FAST_LIMIT = 64 * 1024 * 1024


def call(kernel, out_shape, flops=0, moved=0, **extra):
    return pl.pallas_call(
        kernel,
        out_shape=out_shape,
        compiler_params=pltpu.CompilerParams(vmem_limit_bytes=FAST_LIMIT),
        cost_estimate=pl.CostEstimate(flops=flops, bytes_accessed=moved, transcendentals=0),
        **extra,
    )


VMEM = pl.BlockSpec(memory_space=pltpu.VMEM)
SMEM = pl.BlockSpec(memory_space=pltpu.SMEM)
HBM = pl.BlockSpec(memory_space=pltpu.HBM)
AFTER = pl.BlockSpec(memory_space=pl.ANY)


def own_place():
    token = lax.axis_index("tok")
    return token & 1, lax.shift_right_logical(token, 1)


def fetch(pairs, sems):
    copies = [pltpu.make_async_copy(*pair, sems.at[n]) for n, pair in enumerate(pairs)]
    for copy in copies:
        copy.start()
    return copies


def learner_kernel(gate_hbm, hidden_hbm, delta_hbm, out_ref, gate_ref, hidden_ref, delta_ref, sems):
    copies = fetch([(gate_hbm, gate_ref), (hidden_hbm, hidden_ref), (delta_hbm, delta_ref)], sems)
    peers, _, width = out_ref.shape
    cap = gate_ref.shape[0] // peers
    owned = delta_ref.shape[0]
    copies[0].wait()
    copies[1].wait()
    gate = gate_ref[...].astype(jnp.float32)
    raw = hidden_ref[...].astype(jnp.float32) * gate / (1.0 + jnp.exp(-gate))
    out_ref[:, :cap, :] = raw.astype(jnp.bfloat16).reshape(peers, cap, width)
    copies[2].wait()
    for j in range(delta_ref.shape[1]):
        for k in range(K):
            half = delta_ref[:, j, k, :].astype(jnp.bfloat16)
            for peer in range(k, peers, K):
                out_ref[peer, cap:, j * BLK : (j + 1) * BLK] = half


def place_matrix(target_row, slots):
    rows = target_row.shape[1]
    ids = lax.broadcasted_iota(jnp.int32, (slots, rows), 0)
    return (ids == target_row).astype(jnp.bfloat16)


def as_column(row):
    size = row.shape[1]
    first = lax.broadcasted_iota(jnp.int32, (size, size), 0)
    second = lax.broadcasted_iota(jnp.int32, (size, size), 1)
    return jnp.sum(jnp.where(first == second, row, 0.0), axis=1, keepdims=True)


def weight_of(length_row):
    position = lax.rem(lax.broadcasted_iota(jnp.int32, length_row.shape, 1), RESP)
    return jnp.where(position.astype(jnp.float32) < length_row, RESP / length_row, 0.0)


def sender_kernel(lengths_ref, route_ref, arrived_hbm, out_ref, raw_ref, delta_ref, sems):
    peers, cap, width = raw_ref.shape
    rows = route_ref.shape[1]
    copies = fetch([(arrived_hbm.at[:, :cap, :], raw_ref), (arrived_hbm.at[:, cap:, :], delta_ref)], sems)
    route = route_ref[...]
    named = (lax.broadcasted_iota(jnp.int32, (max(peers, 16), rows), 0) == route).astype(jnp.float32)
    before = (
        lax.broadcasted_iota(jnp.int32, (rows, rows), 0)
        < lax.broadcasted_iota(jnp.int32, (rows, rows), 1)
    ).astype(jnp.bfloat16)
    ranks = jnp.dot(named.astype(jnp.bfloat16), before, preferred_element_type=jnp.float32)
    slot = jnp.sum(named * ranks, axis=0, keepdims=True).astype(jnp.int32)
    target = route * cap + slot
    row_ids = lax.broadcasted_iota(jnp.int32, (1, rows), 1)
    length_row = jnp.zeros((1, rows), jnp.float32)
    for seq in range(rows // RESP):
        mine = (row_ids >= seq * RESP) & (row_ids < (seq + 1) * RESP)
        length_row = jnp.where(mine, lengths_ref[seq].astype(jnp.float32), length_row)
    place = place_matrix(target, peers * cap)
    copies[0].wait()
    raw = raw_ref[...].reshape(peers * cap, width)
    picked = lax.dot_general(
        place, raw, (((0,), (0,)), ((), ())), preferred_element_type=jnp.float32
    )
    out_ref[:rows, :] = (picked * as_column(weight_of(length_row))).astype(jnp.bfloat16)
    out_ref[rows : rows + META, :] = jnp.zeros((META, width), jnp.bfloat16)
    meta_ids = lax.broadcasted_iota(jnp.int32, (META, rows), 0)
    meta = jnp.where(meta_ids == 0, target.astype(jnp.float32), 0.0)
    meta = jnp.where(meta_ids == 1, length_row, meta)
    out_ref[rows : rows + META, :rows] = meta.astype(jnp.bfloat16)
    copies[1].wait()
    out_ref[rows + META :, :] = delta_ref[...].reshape(-1, width)


def gradient_kernel(rows_ref, own_x, mate_x, own_up, mate_up, *refs):
    keep_ref, send_ref, held_ref, x_ref, up_ref, sems = refs
    chips, spots, owned, width = held_ref.shape
    rows = own_x.shape[0]
    pairs = []
    for seat, (x_hbm, up_hbm) in enumerate(((own_x, own_up), (mate_x, mate_up))):
        lines = slice(seat * rows, (seat + 1) * rows)
        pairs.append((up_hbm.at[:rows, :], up_ref.at[lines]))
        for spot in range(spots):
            lanes = pl.ds(pl.multiple_of(rows_ref[spot // K, spot % K] * BLK, BLK), BLK)
            pairs.append((x_hbm.at[:, lanes], x_ref.at[spot, lines]))
    for copy in fetch(pairs, sems):
        copy.wait()
    core, own_chip = own_place()
    for spot in range(spots):
        j = spot // K
        full = lax.dot_general(
            x_ref[spot],
            up_ref[:, j * BLK : (j + 1) * BLK],
            (((0,), (0,)), ((), ())),
            preferred_element_type=jnp.float32,
        ).reshape(chips, 2, owned, width)
        held_ref[:, spot] = jnp.where(core == 0, full[:, 0], full[:, 1]).astype(jnp.bfloat16)
    for number in range(2):
        keep_ref[number] = held_ref[own_chip ^ (2 * number)]
        send_ref[number] = held_ref[own_chip ^ (2 * number + 1)]


def halfway_kernel(keep_ref, came_ref, own_out, send_out):
    own_out[...] = keep_ref[0].astype(jnp.float32) + came_ref[0].astype(jnp.float32)
    send_out[...] = (keep_ref[1].astype(jnp.float32) + came_ref[1].astype(jnp.float32)).astype(jnp.bfloat16)


def adam_kernel(own_ref, came_ref, delta_hbm, m_hbm, v_hbm, *refs):
    delta_out, m_out, v_out, max_out, delta_ref, m_ref, v_ref, sems = refs
    for copy in fetch([(delta_hbm, delta_ref), (m_hbm, m_ref), (v_hbm, v_ref)], sems):
        copy.wait()
    ids = lax.broadcasted_iota(jnp.int32, max_out.shape, 1)
    tops = jnp.zeros(max_out.shape, jnp.float32)
    for j in range(delta_ref.shape[1]):
        for k in range(K):
            spot = j * K + k
            gradient = own_ref[spot] + came_ref[spot].astype(jnp.float32)
            new_m = beta_first * m_ref[:, j, k, :] + (1.0 - beta_first) * gradient
            new_v = beta_second * v_ref[:, j, k, :] + (1.0 - beta_second) * gradient * gradient
            corrected_m = new_m / (1.0 - beta_first**STEP)
            corrected_v = new_v / (1.0 - beta_second**STEP)
            new_delta = delta_ref[:, j, k, :] - step_rate * corrected_m / (
                jnp.sqrt(corrected_v) + adam_eps
            )
            m_out[:, j, k, :] = new_m
            v_out[:, j, k, :] = new_v
            delta_out[:, j, k, :] = new_delta
            tops = jnp.where(ids == spot, jnp.max(jnp.abs(new_delta)), tops)
    high = tops.astype(jnp.bfloat16).astype(jnp.float32)
    middle = (tops - high).astype(jnp.bfloat16).astype(jnp.float32)
    low = tops - high - middle
    kinds = lax.broadcasted_iota(jnp.int32, max_out.shape, 0)
    tops = jnp.where(kinds == 0, high, jnp.where(kinds == 1, middle, low))
    max_out[...] = jnp.where(kinds < 3, tops, 0.0).astype(jnp.bfloat16)


def block_order(core, step):
    return (0, 1 + core, 2 - core, 3)[step]


def scaled(codes_ref, scales_ref, block, spot, lines, lanes):
    return (codes_ref[spot, lines, lanes].astype(jnp.float32) * scales_ref[lanes.start // BLK, block]).astype(
        jnp.bfloat16
    )


def product_kernel(
    scales_ref, rows_ref, own_up, mate_up, own_x, mate_x, *refs
):
    codes_hbm, (sum_ref, *back_refs), (codes, weight, up, delta, x, sems) = refs[:3], refs[3:8], refs[8:]
    rows = own_x.shape[0]
    core, own_chip = own_place()
    turn = own_chip ^ lax.axis_index("col")
    size, width = weight.shape[1:]
    tiles = size // LANE
    pairs = row_pairs(own_up, mate_up, up, delta, core)
    shared = len(pairs)
    starts = []
    for step in range(3):
        first_tile = (2 * (own_chip ^ block_order(core, step)) + core) * tiles
        starts.append(first_tile)
        lanes = pl.ds(pl.multiple_of(first_tile * LANE, LANE), size)
        pairs.append((codes_hbm[step], codes.at[step]))
        pairs.append((own_x.at[:, lanes], x.at[step, :rows]))
        pairs.append((mate_x.at[:, lanes], x.at[step, rows:]))
    copies = fetch(pairs, sems)
    for step in range(3):
        for copy in copies[shared + 3 * step : shared + 3 * (step + 1)]:
            copy.wait()
        for tile in range(tiles):
            block = lax.div(starts[step] + tile, BLK // LANE)
            lines = slice(tile * LANE, (tile + 1) * LANE)
            for j in range(width // BLK):
                lanes = slice(j * BLK, (j + 1) * BLK)
                weight[step, lines, lanes] = scaled(codes, scales_ref, block, step, lines, lanes)
        if step == 0:
            for copy in copies[:shared]:
                copy.wait()
        for j in range(width // BLK):
            lanes = slice(j * BLK, (j + 1) * BLK)
            for k in range(K):
                for piece in range(BLK // LANE):
                    tile = rows_ref[j, k] * (BLK // LANE) + piece - starts[step]

                    @pl.when((tile >= 0) & (tile < tiles))
                    def _():
                        lines = pl.ds(pl.multiple_of(tile * LANE, LANE), LANE)
                        extra = delta[k, piece * LANE : (piece + 1) * LANE, lanes].astype(jnp.float32)
                        held = weight[step, lines, lanes].astype(jnp.float32)
                        weight[step, lines, lanes] = (held + extra).astype(jnp.bfloat16)

        back = lax.dot_general(
            up[...], weight[step], (((1,), (1,)), ((), ())), preferred_element_type=jnp.float32
        ).astype(jnp.bfloat16)
        for shift, back_ref in enumerate(back_refs):

            @pl.when((turn ^ block_order(core, step)) == shift)
            def _():
                back_ref[...] = back

        part_sum = jnp.dot(x[step], weight[step], preferred_element_type=jnp.float32)
        if step == 0:
            sum_ref[...] = part_sum
        else:
            sum_ref[...] += part_sum


def row_pairs(own_up, mate_up, up, delta, core):
    rows = up.shape[0] // 2
    pairs = []
    for seat, up_hbm in enumerate((own_up, mate_up)):
        pairs.append((up_hbm.at[:rows, :], up.at[seat * rows : (seat + 1) * rows]))
        pairs.append((up_hbm.at[rows + META :, :], delta.at[core ^ seat]))
    return pairs


def far_kernel(scales_ref, rows_ref, own_up, mate_up, codes_hbm, *refs):
    weight_out, *back_refs = refs[4:9]
    codes, weight, up, delta, back, sems, out_sems = refs[9:]
    core, own_chip = own_place()
    turn = own_chip ^ lax.axis_index("col")
    size, width = weight.shape
    tiles = size // LANE
    first_tile = (2 * (own_chip ^ 3) + core) * tiles
    copies = fetch([(codes_hbm, codes.at[0])] + row_pairs(own_up, mate_up, up, delta, core), sems)
    copies[0].wait()
    for tile in range(tiles):
        block = lax.div(first_tile + tile, BLK // LANE)
        lines = slice(tile * LANE, (tile + 1) * LANE)
        for j in range(width // BLK):
            lanes = slice(j * BLK, (j + 1) * BLK)
            weight[lines, lanes] = scaled(codes, scales_ref, block, 0, lines, lanes)
    for copy in copies[1:]:
        copy.wait()
    for j in range(width // BLK):
        lanes = slice(j * BLK, (j + 1) * BLK)
        for k in range(K):
            for piece in range(BLK // LANE):
                tile = rows_ref[j, k] * (BLK // LANE) + piece - first_tile

                @pl.when((tile >= 0) & (tile < tiles))
                def _():
                    lines = pl.ds(pl.multiple_of(tile * LANE, LANE), LANE)
                    extra = delta[k, piece * LANE : (piece + 1) * LANE, lanes].astype(jnp.float32)
                    held = weight[lines, lanes].astype(jnp.float32)
                    weight[lines, lanes] = (held + extra).astype(jnp.bfloat16)

    weight_copy = pltpu.make_async_copy(weight, weight_out, out_sems.at[1])
    weight_copy.start()
    back[...] = lax.dot_general(
        up[...], weight[...], (((1,), (1,)), ((), ())), preferred_element_type=jnp.float32
    ).astype(jnp.bfloat16)
    for shift, back_ref in enumerate(back_refs):

        @pl.when((turn ^ 3) == shift)
        def _():
            back_copy = pltpu.make_async_copy(back, back_ref, out_sems.at[0])
            back_copy.start()
            back_copy.wait()

    weight_copy.wait()


def forward_kernel(own_x, mate_x, weight_hbm, sum_hbm, own_out, mate_out, x, weight, total, sems):
    size = weight.shape[0]
    rows = own_out.shape[0]
    core, own_chip = own_place()
    lanes = pl.ds(pl.multiple_of((2 * (own_chip ^ 3) + core) * size, LANE), size)
    pairs = [(own_x.at[:, lanes], x.at[:rows]), (mate_x.at[:, lanes], x.at[rows:])]
    for copy in fetch(pairs + [(weight_hbm, weight), (sum_hbm, total)], sems):
        copy.wait()
    full = total[...] + jnp.dot(x[...], weight[...], preferred_element_type=jnp.float32)
    own_out[...] = full[:rows]
    mate_out[...] = full[rows:]


def spread_up_kernel(own_up, own_sum, other_sum, tops_ref, side_ref, below_ref):
    peers, lines, _ = side_ref.shape
    rows, width = own_sum.shape
    cap, half = lines // 2, width // 2
    target = own_up[rows : rows + META, :rows].astype(jnp.float32)
    place = place_matrix(target[0:1].astype(jnp.int32), peers * cap)
    value = (own_sum[...] + other_sum[...]) * as_column(weight_of(target[1:2]))
    placed = jnp.dot(place, value.astype(jnp.bfloat16), preferred_element_type=jnp.float32)
    placed = placed.astype(jnp.bfloat16).reshape(peers, cap, width)
    for side in range(2):
        side_ref[:, side * cap : (side + 1) * cap, :] = placed[:, :, side * LANE : (side + 1) * LANE]
        below_ref[:, :, side * half : (side + 1) * half] = placed[:, side * META : (side + 1) * META, half:]
    for peer in range(peers):
        below_ref[peer, :, width : width + LANE] = tops_ref[...]
        below_ref[peer, :, width + LANE :] = jnp.zeros((META, below_ref.shape[2] - width - LANE), jnp.bfloat16)


def spread_kernel(own_up, mate_up, up_side, up_below, *refs):
    parts_hbm, out_refs = refs[:4], refs[4:-5]
    held_ref, meta_ref, parts_ref, sems, out_sems = refs[-5:]
    _, rows, size = parts_ref.shape
    rows = rows // 2
    peers = held_ref.shape[0]
    cap = 2 * rows // peers
    core, _ = own_place()
    token = lax.axis_index("tok")
    pairs = [(up.at[rows : rows + META, :rows], meta_ref.at[seat]) for seat, up in enumerate((own_up, mate_up))]
    pairs += [(part, parts_ref.at[n]) for n, part in enumerate(parts_hbm)]
    pairs.append((up_side, held_ref.at[:, : 2 * cap, size:]))
    pairs.append((up_below, held_ref.at[:, 2 * cap :, :]))
    copies = fetch(pairs, sems)
    for copy in copies[:-2]:
        copy.wait()
    for seat in range(2):
        lines = slice(seat * rows, (seat + 1) * rows)
        summed = parts_ref[0, lines].astype(jnp.float32)
        for part in range(1, len(parts_hbm)):
            summed = summed + parts_ref[part, lines].astype(jnp.float32)
        target = meta_ref[seat].astype(jnp.float32)
        place = place_matrix(target[0:1].astype(jnp.int32), peers * cap)
        placed = jnp.dot(place, summed.astype(jnp.bfloat16), preferred_element_type=jnp.float32)
        start = pl.multiple_of((core ^ seat) * cap, cap)
        held_ref[:, pl.ds(start, cap), :size] = placed.astype(jnp.bfloat16).reshape(peers, cap, size)
    copies[-2].wait()
    copies[-1].wait()
    out_copies = fetch([(held_ref.at[token ^ d], far_ref) for d, far_ref in enumerate(out_refs)], out_sems)
    for copy in out_copies:
        copy.wait()


def finish_kernel(gate_hbm, hidden_hbm, delta_hbm, *refs, order):
    arrived_hbm = refs[:-10]
    input_out, gate_out, scale_out, codes_out, gate_ref, hidden_ref, delta_ref, held_ref, sems, out_sems = refs[-10:]
    size = input_out.shape[1] // 2
    peers = len(arrived_hbm)
    cap = gate_ref.shape[0] // peers
    half = gate_ref.shape[1] // 2
    token = lax.axis_index("tok")
    pairs = [(gate_hbm, gate_ref), (hidden_hbm, hidden_ref), (delta_hbm, delta_ref)]
    pairs += [(ref, held_ref.at[number]) for number, ref in enumerate(arrived_hbm)]
    copies = fetch(pairs, sems)
    out_copies = []
    for number, distance in enumerate(order):
        sender = token ^ distance
        lines = pl.ds(pl.multiple_of((sender >> 1) * 2 * cap, 2 * cap), 2 * cap)
        lanes = pl.ds(pl.multiple_of((sender & 1) * size, LANE), size)
        copies[3 + number].wait()
        out_copies.append(
            pltpu.make_async_copy(
                held_ref.at[number, : 2 * cap, :size], input_out.at[lines, lanes], out_sems.at[number]
            )
        )
        out_copies[-1].start()
    for copy in copies[:3]:
        copy.wait()
    tops = jnp.zeros((1, LANE), jnp.float32)
    for number, distance in enumerate(order):
        lines = pl.ds(pl.multiple_of((token ^ distance) * cap, cap), cap)
        held = held_ref.at[number]
        below = [held[2 * cap :, side * half : (side + 1) * half] for side in range(2)]
        value = jnp.concatenate(
            [held[:cap, size:], held[cap : 2 * cap, size:], jnp.concatenate(below, axis=0)], axis=1
        ).astype(jnp.float32)
        gate = gate_ref[lines, :].astype(jnp.float32)
        sigmoid_value = 1.0 / (1.0 + jnp.exp(-gate))
        slope = sigmoid_value * (1.0 + gate * (1.0 - sigmoid_value))
        hidden = hidden_ref[lines, :].astype(jnp.float32)
        gate_out[lines, :] = (hidden * value * slope).astype(jnp.bfloat16)
        kinds = held[2 * cap :, 2 * half : 2 * half + LANE].astype(jnp.float32)
        tops = jnp.maximum(tops, kinds[0:1] + kinds[1:2] + kinds[2:3])
    lanes = lax.broadcasted_iota(jnp.int32, (1, LANE), 1)
    first = lax.broadcasted_iota(jnp.int32, scale_out.shape, 0)
    second = lax.broadcasted_iota(jnp.int32, scale_out.shape, 1)
    scales = jnp.zeros(scale_out.shape, jnp.float32)
    for j in range(delta_ref.shape[1]):
        for k in range(K):
            top = jnp.max(jnp.where(lanes == j * K + k, tops, 0.0))
            scales = jnp.where((first == j) & (second == k), top, scales)
            codes_out[:, j, k, :] = (delta_ref[:, j, k, :] / (top + scale_eps)).astype(jnp.bfloat16)
    scale_out[...] = scales
    for copy in out_copies:
        copy.wait()


def paired(
    peer_count, rollout, lengths, route, up_codes, up_scales, block_rows, delta, adam_m, adam_v, gate_pre, hidden_grad
):
    send_rows, row_width = rollout.shape
    cap = 2 * send_rows // peer_count
    chips = peer_count // 2
    owned = BLK // peer_count
    own_rows, width = up_codes.shape
    mates = [(t, t ^ 1) for t in range(peer_count)]
    scales = up_scales.T
    spots = block_rows.size

    def hop(codes, turned):
        return lax.ppermute(codes, "tok", [(t, t ^ (4 if (t & 1) ^ turned else 2)) for t in range(peer_count)])

    codes_near = hop(up_codes, 0)
    codes_side = hop(up_codes, 1)
    mate_x = lax.ppermute(rollout, "tok", mates)
    first_out = call(
        learner_kernel,
        jax.ShapeDtypeStruct((peer_count, cap + owned, width), jnp.bfloat16),
        in_specs=[HBM] * 3,
        out_specs=VMEM,
        scratch_shapes=[
            pltpu.VMEM(gate_pre.shape, jnp.bfloat16),
            pltpu.VMEM(hidden_grad.shape, jnp.bfloat16),
            pltpu.VMEM(delta.shape, jnp.float32),
            pltpu.SemaphoreType.DMA((3,)),
        ],
    )(gate_pre, hidden_grad, delta)
    arrived = lax.all_to_all(first_out, "tok", split_axis=0, concat_axis=0, tiled=True)
    own_up = call(
        sender_kernel,
        jax.ShapeDtypeStruct((send_rows + META + BLK, width), jnp.bfloat16),
        in_specs=[SMEM, VMEM, HBM],
        out_specs=VMEM,
        scratch_shapes=[
            pltpu.VMEM((peer_count, cap, width), jnp.bfloat16),
            pltpu.VMEM((peer_count, owned, width), jnp.bfloat16),
            pltpu.SemaphoreType.DMA((2,)),
        ],
    )(lengths, route.reshape(1, send_rows), arrived)
    mate_up = lax.ppermute(own_up, "tok", mates)

    codes_far = hop(codes_near, 1)
    back = jax.ShapeDtypeStruct((2 * send_rows, own_rows), jnp.bfloat16)
    row_scratch = [
        pltpu.VMEM((2 * send_rows, width), jnp.bfloat16),
        pltpu.VMEM((K, BLK, width), jnp.bfloat16),
    ]
    early_sum, *backs = call(
        product_kernel,
        [jax.ShapeDtypeStruct((2 * send_rows, width), jnp.float32)] + [back] * chips,
        in_specs=[SMEM] * 2 + [HBM] * 7,
        out_specs=[VMEM] * (1 + chips),
        scratch_shapes=[pltpu.VMEM((3, own_rows, width), jnp.bfloat16)] * 2
        + row_scratch
        + [pltpu.VMEM((3, 2 * send_rows, own_rows), jnp.bfloat16), pltpu.SemaphoreType.DMA((13,))],
    )(scales, block_rows, own_up, mate_up, rollout, mate_x, up_codes, codes_near, codes_side)
    weight_far, *backs = call(
        far_kernel,
        [jax.ShapeDtypeStruct((own_rows, width), jnp.bfloat16)] + [back] * chips,
        in_specs=[SMEM] * 2 + [HBM] * (3 + chips),
        out_specs=[HBM] * (1 + chips),
        scratch_shapes=[
            pltpu.VMEM((1, own_rows, width), jnp.bfloat16),
            pltpu.VMEM((own_rows, width), jnp.bfloat16),
        ]
        + row_scratch
        + [
            pltpu.VMEM(back.shape, jnp.bfloat16),
            pltpu.SemaphoreType.DMA((5,)),
            pltpu.SemaphoreType.DMA((2,)),
        ],
        input_output_aliases={5 + n: 1 + n for n in range(chips)},
    )(scales, block_rows, own_up, mate_up, codes_far, *backs)
    parts = [backs[0]]
    for shift in reversed(range(1, chips)):
        parts.append(lax.ppermute(backs[shift], "col", [(z, z ^ shift) for z in range(chips)]))
    own_sum, mate_sum = call(
        forward_kernel,
        [jax.ShapeDtypeStruct((send_rows, width), jnp.float32)] * 2,
        in_specs=[HBM] * 4,
        out_specs=[VMEM] * 2,
        scratch_shapes=[
            pltpu.VMEM((2 * send_rows, own_rows), jnp.bfloat16),
            pltpu.VMEM((own_rows, width), jnp.bfloat16),
            pltpu.VMEM((2 * send_rows, width), jnp.float32),
            pltpu.SemaphoreType.DMA((4,)),
        ],
    )(rollout, mate_x, weight_far, early_sum)
    other_sum = lax.ppermute(mate_sum, "tok", mates)

    block_pair = jax.ShapeDtypeStruct((2, spots, owned, BLK), jnp.bfloat16)
    kept, leaving = call(
        gradient_kernel,
        [block_pair] * 2,
        in_specs=[SMEM] + [HBM] * 4,
        out_specs=[VMEM] * 2,
        scratch_shapes=[
            pltpu.VMEM((chips, spots, owned, BLK), jnp.bfloat16),
            pltpu.VMEM((spots, 2 * send_rows, BLK), jnp.bfloat16),
            pltpu.VMEM((2 * send_rows, width), jnp.bfloat16),
            pltpu.SemaphoreType.DMA((2 * spots + 2,)),
        ],
    )(block_rows, rollout, mate_x, own_up, mate_up)
    came = lax.ppermute(leaving, "tok", [(t, t ^ 2) for t in range(peer_count)])
    gradient_own, leaving = call(
        halfway_kernel,
        [jax.ShapeDtypeStruct((spots, owned, BLK), dtype) for dtype in (jnp.float32, jnp.bfloat16)],
        in_specs=[VMEM] * 2,
        out_specs=[VMEM] * 2,
    )(kept, came)
    came = lax.ppermute(leaving, "tok", [(t, t ^ 4) for t in range(peer_count)])
    moment = jax.ShapeDtypeStruct(delta.shape, jnp.float32)
    new_delta, new_m, new_v, tops = call(
        adam_kernel,
        (moment, moment, moment, jax.ShapeDtypeStruct((META, LANE), jnp.bfloat16)),
        in_specs=[VMEM] * 2 + [HBM] * 3,
        out_specs=(VMEM,) * 4,
        scratch_shapes=[pltpu.VMEM(delta.shape, jnp.float32)] * 3 + [pltpu.SemaphoreType.DMA((3,))],
    )(gradient_own, came, delta, adam_m, adam_v)

    spread_shape = (2 * cap + META, own_rows + LANE)
    up_side, up_below = call(
        spread_up_kernel,
        [
            jax.ShapeDtypeStruct((peer_count, 2 * cap, LANE), jnp.bfloat16),
            jax.ShapeDtypeStruct((peer_count, META, own_rows + LANE), jnp.bfloat16),
        ],
        in_specs=[VMEM] * 4,
        out_specs=[VMEM] * 2,
    )(own_up, own_sum, other_sum, tops)
    slots = call(
        spread_kernel,
        [jax.ShapeDtypeStruct(spread_shape, jnp.bfloat16)] * peer_count,
        in_specs=[HBM] * (4 + len(parts)),
        out_specs=[HBM] * peer_count,
        scratch_shapes=[
            pltpu.VMEM((peer_count,) + spread_shape, jnp.bfloat16),
            pltpu.VMEM((2, META, send_rows), jnp.bfloat16),
            pltpu.VMEM((len(parts), 2 * send_rows, own_rows), jnp.bfloat16),
            pltpu.SemaphoreType.DMA((4 + len(parts),)),
            pltpu.SemaphoreType.DMA((peer_count,)),
        ],
    )(own_up, mate_up, up_side, up_below, *parts)
    sent = {}
    for distance in sorted(range(1, peer_count), key=lambda d: (-bin(d >> 1).count("1"), d)):
        sent[distance] = lax.ppermute(
            slots[distance], "tok", [(t, t ^ distance) for t in range(peer_count)]
        )
    sent[0] = slots[0]
    order = list(sent)
    input_grad, gate_grad, delta_scale, delta_codes = call(
        functools.partial(finish_kernel, order=order),
        (
            jax.ShapeDtypeStruct((peer_count * cap, 2 * own_rows), jnp.bfloat16),
            jax.ShapeDtypeStruct(gate_pre.shape, jnp.bfloat16),
            jax.ShapeDtypeStruct(block_rows.shape, jnp.float32),
            jax.ShapeDtypeStruct(delta.shape, jnp.bfloat16),
        ),
        in_specs=[HBM] * (3 + peer_count),
        out_specs=(HBM,) + (VMEM,) * 3,
        scratch_shapes=[
            pltpu.VMEM(gate_pre.shape, jnp.bfloat16),
            pltpu.VMEM(hidden_grad.shape, jnp.bfloat16),
            pltpu.VMEM(delta.shape, jnp.float32),
            pltpu.VMEM((peer_count,) + spread_shape, jnp.bfloat16),
            pltpu.SemaphoreType.DMA((3 + peer_count,)),
            pltpu.SemaphoreType.DMA((peer_count,)),
        ],
    )(gate_pre, hidden_grad, new_delta, *[sent[distance] for distance in order])
    return (input_grad, gate_grad, new_delta, new_m, new_v, delta_scale, delta_codes)


def per_device(tok_size, col_size, *arrays):
    rollout, up_codes = arrays[0], arrays[3]
    fits = (
        tok_size == 8 and col_size == 4
        and rollout.shape[0] == LANE
        and up_codes.shape[0] % LANE == 0
        and up_codes.shape[1] == 2 * BLK
    )
    if fits:
        return paired(tok_size, *arrays)
    return any_mesh(*arrays)


def solution(mesh):
    placed = (
        P("tok", None),
        P("tok"),
        P("tok", None),
        P("tok", "col"),
        P(None, "col"),
        P("col", None),
        P("tok", "col", None, None),
        P("tok", "col", None, None),
        P("tok", "col", None, None),
        P("tok", "col"),
        P("tok", "col"),
    )
    return jax.shard_map(
        functools.partial(per_device, mesh.shape["tok"], mesh.shape["col"]),
        mesh=mesh,
        in_specs=placed,
        out_specs=(
            P("tok", "col"),
            P("tok", "col"),
            P("tok", "col", None, None),
            P("tok", "col", None, None),
            P("tok", "col", None, None),
            P("col", None),
            P("tok", "col", None, None),
        ),
        check_vma=False,
    )
```

```python
import functools

import jax
import jax.numpy as jnp
from jax import lax
from jax.experimental import pallas as pl
from jax.experimental.pallas import tpu as pltpu
from jax.sharding import PartitionSpec as P

BLK = 256
K = 2
RESP = 64
STEP = 1000


beta_first = 0.9
beta_second = 0.999
step_rate = 0.01
adam_eps = 1e-08
scale_eps = 1e-06


def silu_slope(operand):
    sigmoid_value = jax.nn.sigmoid(operand)
    return sigmoid_value * (1.0 + operand * (1.0 - sigmoid_value))


def dequant(code_rows, scales):
    row_count = code_rows.shape[0]
    block_count = scales.shape[0]
    width_blocks = scales.shape[1]
    block_of_row = jnp.arange(row_count, dtype=jnp.int32) // BLK
    selector = (block_of_row[:, None] == jnp.arange(block_count, dtype=jnp.int32)[None, :]).astype(
        jnp.float32
    )
    row_scales = jnp.dot(selector, scales, precision=lax.Precision.HIGHEST)
    spread = (
        code_rows.astype(jnp.float32).reshape(row_count, width_blocks, -1) * row_scales[:, :, None]
    )
    return spread.reshape(row_count, -1).astype(jnp.bfloat16)


def any_mesh(
    rollout,
    lengths,
    route,
    up_codes,
    up_scales,
    block_rows,
    delta,
    adam_m,
    adam_v,
    gate_pre,
    hidden_grad,
):
    peer_count = lax.axis_size("tok")
    send_rows = rollout.shape[0]
    row_width = rollout.shape[1]
    capacity = 2 * send_rows // peer_count
    row_ids = jnp.arange(send_rows, dtype=jnp.int32)
    seq_len = jnp.repeat(lengths, RESP)
    position = row_ids % RESP
    row_weight = jnp.where(position < seq_len, RESP / seq_len.astype(jnp.float32), 0.0)
    destination = route[:, 0]
    onehot = (destination[:, None] == jnp.arange(peer_count, dtype=jnp.int32)[None, :]).astype(
        jnp.int32
    )
    slot_index = jnp.sum((jnp.cumsum(onehot, axis=0) - 1) * onehot, axis=1)
    target = destination * capacity + slot_index
    weight_slots = (
        jnp.zeros((peer_count * capacity,), jnp.float32)
        .at[target]
        .set(row_weight)
        .reshape(peer_count, capacity)
    )
    buffer = (
        jnp.zeros((peer_count * capacity, row_width), jnp.bfloat16)
        .at[target]
        .set(rollout)
        .reshape(peer_count, capacity, row_width)
    )
    arrived, arrived_weight = (
        lax.all_to_all(buffer, "tok", split_axis=0, concat_axis=0, tiled=True),
        lax.all_to_all(
            weight_slots.astype(jnp.bfloat16), "tok", split_axis=0, concat_axis=0, tiled=True
        ).astype(weight_slots.dtype),
    )
    learn_x = arrived.reshape(peer_count * capacity, row_width)
    learn_w = arrived_weight.reshape(peer_count * capacity)
    rows_learn = learn_x.shape[0]
    column_count = up_codes.shape[1]
    blocks_here = column_count // BLK
    block_total = up_scales.shape[0]
    delta_full = lax.all_gather(delta.astype(jnp.bfloat16), "tok", axis=0, tiled=True)
    chosen = jnp.take(
        learn_x.reshape(rows_learn, block_total, BLK), block_rows.reshape(-1), axis=1
    ).reshape(rows_learn, blocks_here, K, BLK)
    activation = jax.nn.silu(gate_pre.astype(jnp.float32))
    up_grad = (hidden_grad.astype(jnp.float32) * activation * learn_w[:, None]).astype(jnp.bfloat16)
    up_grad_blocks = up_grad.reshape(rows_learn, blocks_here, BLK)
    delta_up = jnp.einsum(
        "rjkb,bjkc->rjc", chosen, delta_full, preferred_element_type=jnp.float32
    ).reshape(rows_learn, column_count)
    delta_back = jnp.einsum(
        "rjc,bjkc->rjkb", up_grad_blocks, delta_full, preferred_element_type=jnp.float32
    )
    selector = (
        block_rows.reshape(-1)[:, None] == jnp.arange(block_total, dtype=jnp.int32)[None, :]
    ).astype(jnp.float32)
    delta_input = jnp.einsum(
        "rqb,qd->rdb",
        delta_back.reshape(rows_learn, -1, BLK),
        selector,
        precision=lax.Precision.HIGHEST,
    ).reshape(rows_learn, row_width)
    weight = dequant(lax.all_gather(up_codes, "tok", axis=0, tiled=True), up_scales)
    base_up = jnp.dot(learn_x, weight, preferred_element_type=jnp.float32)
    weight = dequant(lax.all_gather(up_codes, "tok", axis=0, tiled=True), up_scales)
    base_input = lax.dot_general(
        up_grad, weight, (((1,), (1,)), ((), ())), preferred_element_type=jnp.float32
    )
    up_value = base_up + delta_up
    gate_grad = (
        hidden_grad.astype(jnp.float32)
        * up_value
        * silu_slope(gate_pre.astype(jnp.float32))
        * learn_w[:, None]
    ).astype(jnp.bfloat16)
    input_grad = lax.psum_scatter(
        base_input + delta_input, "col", scatter_dimension=1, tiled=True
    ).astype(jnp.bfloat16)
    owned_rows = BLK // peer_count
    summed_grad = lax.psum(
        jnp.einsum("rjkb,rjc->bjkc", chosen, up_grad_blocks, preferred_element_type=jnp.float32),
        "tok",
    )
    gradient = lax.dynamic_slice_in_dim(
        summed_grad, lax.axis_index("tok") * owned_rows, owned_rows, 0
    )
    new_m = beta_first * adam_m + (1.0 - beta_first) * gradient
    new_v = beta_second * adam_v + (1.0 - beta_second) * gradient * gradient
    corrected_m = new_m / (1.0 - beta_first**STEP)
    corrected_v = new_v / (1.0 - beta_second**STEP)
    new_delta = delta - step_rate * corrected_m / (jnp.sqrt(corrected_v) + adam_eps)
    local_max = jnp.max(jnp.abs(new_delta), axis=(0, 3))
    block_scale = lax.pmax(local_max, "tok")
    new_codes = (new_delta / (block_scale + scale_eps)[None, :, :, None]).astype(jnp.bfloat16)
    return (input_grad, gate_grad, new_delta, new_m, new_v, block_scale, new_codes)


LANE = 128
META = 16
FAST_LIMIT = 64 * 1024 * 1024


def call(kernel, out_shape, flops=0, moved=0, **extra):
    return pl.pallas_call(
        kernel,
        out_shape=out_shape,
        compiler_params=pltpu.CompilerParams(vmem_limit_bytes=FAST_LIMIT),
        cost_estimate=pl.CostEstimate(flops=flops, bytes_accessed=moved, transcendentals=0),
        **extra,
    )


VMEM = pl.BlockSpec(memory_space=pltpu.VMEM)
SMEM = pl.BlockSpec(memory_space=pltpu.SMEM)
HBM = pl.BlockSpec(memory_space=pltpu.HBM)
AFTER = pl.BlockSpec(memory_space=pl.ANY)


def own_place():
    token = lax.axis_index("tok")
    return token & 1, lax.shift_right_logical(token, 1)


def fetch(pairs, sems):
    copies = [pltpu.make_async_copy(*pair, sems.at[n]) for n, pair in enumerate(pairs)]
    for copy in copies:
        copy.start()
    return copies


def learner_kernel(gate_hbm, hidden_hbm, delta_hbm, out_ref, gate_ref, hidden_ref, delta_ref, sems):
    copies = fetch([(gate_hbm, gate_ref), (hidden_hbm, hidden_ref), (delta_hbm, delta_ref)], sems)
    peers, _, width = out_ref.shape
    cap = gate_ref.shape[0] // peers
    owned = delta_ref.shape[0]
    copies[0].wait()
    copies[1].wait()
    gate = gate_ref[...].astype(jnp.float32)
    raw = hidden_ref[...].astype(jnp.float32) * gate / (1.0 + jnp.exp(-gate))
    out_ref[:, :cap, :] = raw.astype(jnp.bfloat16).reshape(peers, cap, width)
    copies[2].wait()
    for j in range(delta_ref.shape[1]):
        for k in range(K):
            half = delta_ref[:, j, k, :].astype(jnp.bfloat16)
            for peer in range(k, peers, K):
                out_ref[peer, cap:, j * BLK : (j + 1) * BLK] = half


def place_matrix(target_row, slots):
    rows = target_row.shape[1]
    ids = lax.broadcasted_iota(jnp.int32, (slots, rows), 0)
    return (ids == target_row).astype(jnp.bfloat16)


def as_column(row):
    size = row.shape[1]
    first = lax.broadcasted_iota(jnp.int32, (size, size), 0)
    second = lax.broadcasted_iota(jnp.int32, (size, size), 1)
    return jnp.sum(jnp.where(first == second, row, 0.0), axis=1, keepdims=True)


def weight_of(length_row):
    position = lax.rem(lax.broadcasted_iota(jnp.int32, length_row.shape, 1), RESP)
    return jnp.where(position.astype(jnp.float32) < length_row, RESP / length_row, 0.0)


def sender_kernel(lengths_ref, route_ref, arrived_hbm, out_ref, raw_ref, delta_ref, sems):
    peers, cap, width = raw_ref.shape
    rows = route_ref.shape[1]
    copies = fetch([(arrived_hbm.at[:, :cap, :], raw_ref), (arrived_hbm.at[:, cap:, :], delta_ref)], sems)
    route = route_ref[...]
    named = (lax.broadcasted_iota(jnp.int32, (max(peers, 16), rows), 0) == route).astype(jnp.float32)
    before = (
        lax.broadcasted_iota(jnp.int32, (rows, rows), 0)
        < lax.broadcasted_iota(jnp.int32, (rows, rows), 1)
    ).astype(jnp.bfloat16)
    ranks = jnp.dot(named.astype(jnp.bfloat16), before, preferred_element_type=jnp.float32)
    slot = jnp.sum(named * ranks, axis=0, keepdims=True).astype(jnp.int32)
    target = route * cap + slot
    row_ids = lax.broadcasted_iota(jnp.int32, (1, rows), 1)
    length_row = jnp.zeros((1, rows), jnp.float32)
    for seq in range(rows // RESP):
        mine = (row_ids >= seq * RESP) & (row_ids < (seq + 1) * RESP)
        length_row = jnp.where(mine, lengths_ref[seq].astype(jnp.float32), length_row)
    place = place_matrix(target, peers * cap)
    copies[0].wait()
    raw = raw_ref[...].reshape(peers * cap, width)
    picked = lax.dot_general(
        place, raw, (((0,), (0,)), ((), ())), preferred_element_type=jnp.float32
    )
    out_ref[:rows, :] = (picked * as_column(weight_of(length_row))).astype(jnp.bfloat16)
    out_ref[rows : rows + META, :] = jnp.zeros((META, width), jnp.bfloat16)
    meta_ids = lax.broadcasted_iota(jnp.int32, (META, rows), 0)
    meta = jnp.where(meta_ids == 0, target.astype(jnp.float32), 0.0)
    meta = jnp.where(meta_ids == 1, length_row, meta)
    out_ref[rows : rows + META, :rows] = meta.astype(jnp.bfloat16)
    copies[1].wait()
    out_ref[rows + META :, :] = delta_ref[...].reshape(-1, width)


def gradient_kernel(rows_ref, own_x, mate_x, own_up, mate_up, *refs):
    out_refs, (held_ref, x_ref, up_ref, sems) = refs[:-4], refs[-4:]
    chips, spots, owned, width = held_ref.shape
    rows = own_x.shape[0]
    pairs = []
    for seat, (x_hbm, up_hbm) in enumerate(((own_x, own_up), (mate_x, mate_up))):
        lines = slice(seat * rows, (seat + 1) * rows)
        pairs.append((up_hbm.at[:rows, :], up_ref.at[lines]))
        for spot in range(spots):
            lanes = pl.ds(pl.multiple_of(rows_ref[spot // K, spot % K] * BLK, BLK), BLK)
            pairs.append((x_hbm.at[:, lanes], x_ref.at[spot, lines]))
    for copy in fetch(pairs, sems):
        copy.wait()
    core, own_chip = own_place()
    for spot in range(spots):
        j = spot // K
        full = lax.dot_general(
            x_ref[spot],
            up_ref[:, j * BLK : (j + 1) * BLK],
            (((0,), (0,)), ((), ())),
            preferred_element_type=jnp.float32,
        ).reshape(chips, 2, owned, width)
        held_ref[:, spot] = jnp.where(core == 0, full[:, 0], full[:, 1]).astype(jnp.bfloat16)
    for distance, out_ref in enumerate(out_refs):
        out_ref[...] = held_ref[own_chip ^ distance]


def adam_kernel(delta_hbm, m_hbm, v_hbm, *refs):
    delta_out, m_out, v_out, max_out, delta_ref, m_ref, v_ref, grad_ref, sems = refs[-9:]
    chips = grad_ref.shape[0]
    pairs = [(delta_hbm, delta_ref), (m_hbm, m_ref), (v_hbm, v_ref)]
    for copy in fetch(pairs + [(refs[chip], grad_ref.at[chip]) for chip in range(chips)], sems):
        copy.wait()
    ids = lax.broadcasted_iota(jnp.int32, max_out.shape, 1)
    tops = jnp.zeros(max_out.shape, jnp.float32)
    for j in range(delta_ref.shape[1]):
        for k in range(K):
            spot = j * K + k
            gradient = grad_ref[0, spot].astype(jnp.float32)
            for chip in range(1, chips):
                gradient = gradient + grad_ref[chip, spot].astype(jnp.float32)
            new_m = beta_first * m_ref[:, j, k, :] + (1.0 - beta_first) * gradient
            new_v = beta_second * v_ref[:, j, k, :] + (1.0 - beta_second) * gradient * gradient
            corrected_m = new_m / (1.0 - beta_first**STEP)
            corrected_v = new_v / (1.0 - beta_second**STEP)
            new_delta = delta_ref[:, j, k, :] - step_rate * corrected_m / (
                jnp.sqrt(corrected_v) + adam_eps
            )
            m_out[:, j, k, :] = new_m
            v_out[:, j, k, :] = new_v
            delta_out[:, j, k, :] = new_delta
            tops = jnp.where(ids == spot, jnp.max(jnp.abs(new_delta)), tops)
    high = tops.astype(jnp.bfloat16).astype(jnp.float32)
    middle = (tops - high).astype(jnp.bfloat16).astype(jnp.float32)
    low = tops - high - middle
    kinds = lax.broadcasted_iota(jnp.int32, max_out.shape, 0)
    tops = jnp.where(kinds == 0, high, jnp.where(kinds == 1, middle, low))
    max_out[...] = jnp.where(kinds < 3, tops, 0.0).astype(jnp.bfloat16)


def block_order(core, step):
    return (0, 1 + core, 2 - core, 3)[step]


def scaled(codes_ref, scales_ref, block, spot, lines, lanes):
    return (codes_ref[spot, lines, lanes].astype(jnp.float32) * scales_ref[lanes.start // BLK, block]).astype(
        jnp.bfloat16
    )


def product_kernel(
    scales_ref, rows_ref, own_up, mate_up, own_x, mate_x, *refs
):
    codes_hbm, (sum_ref, *back_refs), (codes, weight, up, delta, x, sems) = refs[:3], refs[3:8], refs[8:]
    rows = own_x.shape[0]
    core, own_chip = own_place()
    turn = own_chip ^ lax.axis_index("col")
    size, width = weight.shape[1:]
    tiles = size // LANE
    pairs = row_pairs(own_up, mate_up, up, delta, core)
    shared = len(pairs)
    starts = []
    for step in range(3):
        first_tile = (2 * (own_chip ^ block_order(core, step)) + core) * tiles
        starts.append(first_tile)
        lanes = pl.ds(pl.multiple_of(first_tile * LANE, LANE), size)
        pairs.append((codes_hbm[step], codes.at[step]))
        pairs.append((own_x.at[:, lanes], x.at[step, :rows]))
        pairs.append((mate_x.at[:, lanes], x.at[step, rows:]))
    copies = fetch(pairs, sems)
    for step in range(3):
        for copy in copies[shared + 3 * step : shared + 3 * (step + 1)]:
            copy.wait()
        for tile in range(tiles):
            block = lax.div(starts[step] + tile, BLK // LANE)
            lines = slice(tile * LANE, (tile + 1) * LANE)
            for j in range(width // BLK):
                lanes = slice(j * BLK, (j + 1) * BLK)
                weight[step, lines, lanes] = scaled(codes, scales_ref, block, step, lines, lanes)
        if step == 0:
            for copy in copies[:shared]:
                copy.wait()
        for j in range(width // BLK):
            lanes = slice(j * BLK, (j + 1) * BLK)
            for k in range(K):
                for piece in range(BLK // LANE):
                    tile = rows_ref[j, k] * (BLK // LANE) + piece - starts[step]

                    @pl.when((tile >= 0) & (tile < tiles))
                    def _():
                        lines = pl.ds(pl.multiple_of(tile * LANE, LANE), LANE)
                        extra = delta[k, piece * LANE : (piece + 1) * LANE, lanes].astype(jnp.float32)
                        held = weight[step, lines, lanes].astype(jnp.float32)
                        weight[step, lines, lanes] = (held + extra).astype(jnp.bfloat16)

        back = lax.dot_general(
            up[...], weight[step], (((1,), (1,)), ((), ())), preferred_element_type=jnp.float32
        ).astype(jnp.bfloat16)
        for shift, back_ref in enumerate(back_refs):

            @pl.when((turn ^ block_order(core, step)) == shift)
            def _():
                back_ref[...] = back

        part_sum = jnp.dot(x[step], weight[step], preferred_element_type=jnp.float32)
        if step == 0:
            sum_ref[...] = part_sum
        else:
            sum_ref[...] += part_sum


def row_pairs(own_up, mate_up, up, delta, core):
    rows = up.shape[0] // 2
    pairs = []
    for seat, up_hbm in enumerate((own_up, mate_up)):
        pairs.append((up_hbm.at[:rows, :], up.at[seat * rows : (seat + 1) * rows]))
        pairs.append((up_hbm.at[rows + META :, :], delta.at[core ^ seat]))
    return pairs


def far_kernel(scales_ref, rows_ref, own_up, mate_up, codes_hbm, *refs):
    weight_out, *back_refs = refs[4:9]
    codes, weight, up, delta, back, sems, out_sems = refs[9:]
    core, own_chip = own_place()
    turn = own_chip ^ lax.axis_index("col")
    size, width = weight.shape
    tiles = size // LANE
    first_tile = (2 * (own_chip ^ 3) + core) * tiles
    copies = fetch([(codes_hbm, codes.at[0])] + row_pairs(own_up, mate_up, up, delta, core), sems)
    copies[0].wait()
    for tile in range(tiles):
        block = lax.div(first_tile + tile, BLK // LANE)
        lines = slice(tile * LANE, (tile + 1) * LANE)
        for j in range(width // BLK):
            lanes = slice(j * BLK, (j + 1) * BLK)
            weight[lines, lanes] = scaled(codes, scales_ref, block, 0, lines, lanes)
    for copy in copies[1:]:
        copy.wait()
    for j in range(width // BLK):
        lanes = slice(j * BLK, (j + 1) * BLK)
        for k in range(K):
            for piece in range(BLK // LANE):
                tile = rows_ref[j, k] * (BLK // LANE) + piece - first_tile

                @pl.when((tile >= 0) & (tile < tiles))
                def _():
                    lines = pl.ds(pl.multiple_of(tile * LANE, LANE), LANE)
                    extra = delta[k, piece * LANE : (piece + 1) * LANE, lanes].astype(jnp.float32)
                    held = weight[lines, lanes].astype(jnp.float32)
                    weight[lines, lanes] = (held + extra).astype(jnp.bfloat16)

    weight_copy = pltpu.make_async_copy(weight, weight_out, out_sems.at[1])
    weight_copy.start()
    back[...] = lax.dot_general(
        up[...], weight[...], (((1,), (1,)), ((), ())), preferred_element_type=jnp.float32
    ).astype(jnp.bfloat16)
    for shift, back_ref in enumerate(back_refs):

        @pl.when((turn ^ 3) == shift)
        def _():
            back_copy = pltpu.make_async_copy(back, back_ref, out_sems.at[0])
            back_copy.start()
            back_copy.wait()

    weight_copy.wait()


def forward_kernel(own_x, mate_x, weight_hbm, sum_hbm, own_out, mate_out, x, weight, total, sems):
    size = weight.shape[0]
    rows = own_out.shape[0]
    core, own_chip = own_place()
    lanes = pl.ds(pl.multiple_of((2 * (own_chip ^ 3) + core) * size, LANE), size)
    pairs = [(own_x.at[:, lanes], x.at[:rows]), (mate_x.at[:, lanes], x.at[rows:])]
    for copy in fetch(pairs + [(weight_hbm, weight), (sum_hbm, total)], sems):
        copy.wait()
    full = total[...] + jnp.dot(x[...], weight[...], preferred_element_type=jnp.float32)
    own_out[...] = full[:rows]
    mate_out[...] = full[rows:]


def spread_up_kernel(own_up, own_sum, other_sum, tops_ref, side_ref, below_ref):
    peers, lines, _ = side_ref.shape
    rows, width = own_sum.shape
    cap, half = lines // 2, width // 2
    target = own_up[rows : rows + META, :rows].astype(jnp.float32)
    place = place_matrix(target[0:1].astype(jnp.int32), peers * cap)
    value = (own_sum[...] + other_sum[...]) * as_column(weight_of(target[1:2]))
    placed = jnp.dot(place, value.astype(jnp.bfloat16), preferred_element_type=jnp.float32)
    placed = placed.astype(jnp.bfloat16).reshape(peers, cap, width)
    for side in range(2):
        side_ref[:, side * cap : (side + 1) * cap, :] = placed[:, :, side * LANE : (side + 1) * LANE]
        below_ref[:, :, side * half : (side + 1) * half] = placed[:, side * META : (side + 1) * META, half:]
    for peer in range(peers):
        below_ref[peer, :, width : width + LANE] = tops_ref[...]
        below_ref[peer, :, width + LANE :] = jnp.zeros((META, below_ref.shape[2] - width - LANE), jnp.bfloat16)


def spread_kernel(own_up, mate_up, up_side, up_below, *refs):
    parts_hbm, out_refs = refs[:4], refs[4:-5]
    held_ref, meta_ref, parts_ref, sems, out_sems = refs[-5:]
    _, rows, size = parts_ref.shape
    rows = rows // 2
    peers = held_ref.shape[0]
    cap = 2 * rows // peers
    core, _ = own_place()
    token = lax.axis_index("tok")
    pairs = [(up.at[rows : rows + META, :rows], meta_ref.at[seat]) for seat, up in enumerate((own_up, mate_up))]
    pairs += [(part, parts_ref.at[n]) for n, part in enumerate(parts_hbm)]
    pairs.append((up_side, held_ref.at[:, : 2 * cap, size:]))
    pairs.append((up_below, held_ref.at[:, 2 * cap :, :]))
    copies = fetch(pairs, sems)
    for copy in copies[:-2]:
        copy.wait()
    for seat in range(2):
        lines = slice(seat * rows, (seat + 1) * rows)
        summed = parts_ref[0, lines].astype(jnp.float32)
        for part in range(1, len(parts_hbm)):
            summed = summed + parts_ref[part, lines].astype(jnp.float32)
        target = meta_ref[seat].astype(jnp.float32)
        place = place_matrix(target[0:1].astype(jnp.int32), peers * cap)
        placed = jnp.dot(place, summed.astype(jnp.bfloat16), preferred_element_type=jnp.float32)
        start = pl.multiple_of((core ^ seat) * cap, cap)
        held_ref[:, pl.ds(start, cap), :size] = placed.astype(jnp.bfloat16).reshape(peers, cap, size)
    copies[-2].wait()
    copies[-1].wait()
    out_copies = fetch([(held_ref.at[token ^ d], far_ref) for d, far_ref in enumerate(out_refs)], out_sems)
    for copy in out_copies:
        copy.wait()


def finish_kernel(gate_hbm, hidden_hbm, delta_hbm, *refs, order):
    arrived_hbm = refs[:-10]
    input_out, gate_out, scale_out, codes_out, gate_ref, hidden_ref, delta_ref, held_ref, sems, out_sems = refs[-10:]
    size = input_out.shape[1] // 2
    peers = len(arrived_hbm)
    cap = gate_ref.shape[0] // peers
    half = gate_ref.shape[1] // 2
    token = lax.axis_index("tok")
    pairs = [(gate_hbm, gate_ref), (hidden_hbm, hidden_ref), (delta_hbm, delta_ref)]
    pairs += [(ref, held_ref.at[number]) for number, ref in enumerate(arrived_hbm)]
    copies = fetch(pairs, sems)
    out_copies = []
    for number, distance in enumerate(order):
        sender = token ^ distance
        lines = pl.ds(pl.multiple_of((sender >> 1) * 2 * cap, 2 * cap), 2 * cap)
        lanes = pl.ds(pl.multiple_of((sender & 1) * size, LANE), size)
        copies[3 + number].wait()
        out_copies.append(
            pltpu.make_async_copy(
                held_ref.at[number, : 2 * cap, :size], input_out.at[lines, lanes], out_sems.at[number]
            )
        )
        out_copies[-1].start()
    for copy in copies[:3]:
        copy.wait()
    tops = jnp.zeros((1, LANE), jnp.float32)
    for number, distance in enumerate(order):
        lines = pl.ds(pl.multiple_of((token ^ distance) * cap, cap), cap)
        held = held_ref.at[number]
        below = [held[2 * cap :, side * half : (side + 1) * half] for side in range(2)]
        value = jnp.concatenate(
            [held[:cap, size:], held[cap : 2 * cap, size:], jnp.concatenate(below, axis=0)], axis=1
        ).astype(jnp.float32)
        gate = gate_ref[lines, :].astype(jnp.float32)
        sigmoid_value = 1.0 / (1.0 + jnp.exp(-gate))
        slope = sigmoid_value * (1.0 + gate * (1.0 - sigmoid_value))
        hidden = hidden_ref[lines, :].astype(jnp.float32)
        gate_out[lines, :] = (hidden * value * slope).astype(jnp.bfloat16)
        kinds = held[2 * cap :, 2 * half : 2 * half + LANE].astype(jnp.float32)
        tops = jnp.maximum(tops, kinds[0:1] + kinds[1:2] + kinds[2:3])
    lanes = lax.broadcasted_iota(jnp.int32, (1, LANE), 1)
    first = lax.broadcasted_iota(jnp.int32, scale_out.shape, 0)
    second = lax.broadcasted_iota(jnp.int32, scale_out.shape, 1)
    scales = jnp.zeros(scale_out.shape, jnp.float32)
    for j in range(delta_ref.shape[1]):
        for k in range(K):
            top = jnp.max(jnp.where(lanes == j * K + k, tops, 0.0))
            scales = jnp.where((first == j) & (second == k), top, scales)
            codes_out[:, j, k, :] = (delta_ref[:, j, k, :] / (top + scale_eps)).astype(jnp.bfloat16)
    scale_out[...] = scales
    for copy in out_copies:
        copy.wait()


def paired(
    peer_count, rollout, lengths, route, up_codes, up_scales, block_rows, delta, adam_m, adam_v, gate_pre, hidden_grad
):
    send_rows, row_width = rollout.shape
    cap = 2 * send_rows // peer_count
    chips = peer_count // 2
    owned = BLK // peer_count
    own_rows, width = up_codes.shape
    mates = [(t, t ^ 1) for t in range(peer_count)]
    scales = up_scales.T
    spots = block_rows.size

    def hop(codes, turned):
        return lax.ppermute(codes, "tok", [(t, t ^ (4 if (t & 1) ^ turned else 2)) for t in range(peer_count)])

    codes_near = hop(up_codes, 0)
    codes_side = hop(up_codes, 1)
    mate_x = lax.ppermute(rollout, "tok", mates)
    first_out = call(
        learner_kernel,
        jax.ShapeDtypeStruct((peer_count, cap + owned, width), jnp.bfloat16),
        in_specs=[HBM] * 3,
        out_specs=VMEM,
        scratch_shapes=[
            pltpu.VMEM(gate_pre.shape, jnp.bfloat16),
            pltpu.VMEM(hidden_grad.shape, jnp.bfloat16),
            pltpu.VMEM(delta.shape, jnp.float32),
            pltpu.SemaphoreType.DMA((3,)),
        ],
    )(gate_pre, hidden_grad, delta)
    arrived = lax.all_to_all(first_out, "tok", split_axis=0, concat_axis=0, tiled=True)
    own_up = call(
        sender_kernel,
        jax.ShapeDtypeStruct((send_rows + META + BLK, width), jnp.bfloat16),
        in_specs=[SMEM, VMEM, HBM],
        out_specs=VMEM,
        scratch_shapes=[
            pltpu.VMEM((peer_count, cap, width), jnp.bfloat16),
            pltpu.VMEM((peer_count, owned, width), jnp.bfloat16),
            pltpu.SemaphoreType.DMA((2,)),
        ],
    )(lengths, route.reshape(1, send_rows), arrived)
    mate_up = lax.ppermute(own_up, "tok", mates)

    codes_far = hop(codes_near, 1)
    back = jax.ShapeDtypeStruct((2 * send_rows, own_rows), jnp.bfloat16)
    row_scratch = [
        pltpu.VMEM((2 * send_rows, width), jnp.bfloat16),
        pltpu.VMEM((K, BLK, width), jnp.bfloat16),
    ]
    early_sum, *backs = call(
        product_kernel,
        [jax.ShapeDtypeStruct((2 * send_rows, width), jnp.float32)] + [back] * chips,
        in_specs=[SMEM] * 2 + [HBM] * 7,
        out_specs=[VMEM] * (1 + chips),
        scratch_shapes=[pltpu.VMEM((3, own_rows, width), jnp.bfloat16)] * 2
        + row_scratch
        + [pltpu.VMEM((3, 2 * send_rows, own_rows), jnp.bfloat16), pltpu.SemaphoreType.DMA((13,))],
    )(scales, block_rows, own_up, mate_up, rollout, mate_x, up_codes, codes_near, codes_side)
    weight_far, *backs = call(
        far_kernel,
        [jax.ShapeDtypeStruct((own_rows, width), jnp.bfloat16)] + [back] * chips,
        in_specs=[SMEM] * 2 + [HBM] * (3 + chips),
        out_specs=[HBM] * (1 + chips),
        scratch_shapes=[
            pltpu.VMEM((1, own_rows, width), jnp.bfloat16),
            pltpu.VMEM((own_rows, width), jnp.bfloat16),
        ]
        + row_scratch
        + [
            pltpu.VMEM(back.shape, jnp.bfloat16),
            pltpu.SemaphoreType.DMA((5,)),
            pltpu.SemaphoreType.DMA((2,)),
        ],
        input_output_aliases={5 + n: 1 + n for n in range(chips)},
    )(scales, block_rows, own_up, mate_up, codes_far, *backs)
    parts = [backs[0]]
    for shift in range(1, chips):
        parts.append(lax.ppermute(backs[shift], "col", [(z, z ^ shift) for z in range(chips)]))
    own_sum, mate_sum = call(
        forward_kernel,
        [jax.ShapeDtypeStruct((send_rows, width), jnp.float32)] * 2,
        in_specs=[HBM] * 4,
        out_specs=[VMEM] * 2,
        scratch_shapes=[
            pltpu.VMEM((2 * send_rows, own_rows), jnp.bfloat16),
            pltpu.VMEM((own_rows, width), jnp.bfloat16),
            pltpu.VMEM((2 * send_rows, width), jnp.float32),
            pltpu.SemaphoreType.DMA((4,)),
        ],
    )(rollout, mate_x, weight_far, early_sum)
    other_sum = lax.ppermute(mate_sum, "tok", mates)

    gradient_parts = call(
        gradient_kernel,
        [jax.ShapeDtypeStruct((spots, owned, BLK), jnp.bfloat16)] * chips,
        in_specs=[SMEM] + [HBM] * 4,
        out_specs=[VMEM] * chips,
        scratch_shapes=[
            pltpu.VMEM((chips, spots, owned, BLK), jnp.bfloat16),
            pltpu.VMEM((spots, 2 * send_rows, BLK), jnp.bfloat16),
            pltpu.VMEM((2 * send_rows, width), jnp.bfloat16),
            pltpu.SemaphoreType.DMA((2 * spots + 2,)),
        ],
    )(block_rows, rollout, mate_x, own_up, mate_up)
    gradient_arrived = [gradient_parts[0]] + [
        lax.ppermute(gradient_parts[step], "tok", [(t, t ^ (2 * step)) for t in range(peer_count)])
        for step in range(1, chips)
    ]
    moment = jax.ShapeDtypeStruct(delta.shape, jnp.float32)
    new_delta, new_m, new_v, tops = call(
        adam_kernel,
        (moment, moment, moment, jax.ShapeDtypeStruct((META, LANE), jnp.bfloat16)),
        in_specs=[HBM] * (3 + chips),
        out_specs=(VMEM,) * 4,
        scratch_shapes=[pltpu.VMEM(delta.shape, jnp.float32)] * 3
        + [pltpu.VMEM((chips, spots, owned, BLK), jnp.bfloat16), pltpu.SemaphoreType.DMA((3 + chips,))],
    )(delta, adam_m, adam_v, *gradient_arrived)

    spread_shape = (2 * cap + META, own_rows + LANE)
    up_side, up_below = call(
        spread_up_kernel,
        [
            jax.ShapeDtypeStruct((peer_count, 2 * cap, LANE), jnp.bfloat16),
            jax.ShapeDtypeStruct((peer_count, META, own_rows + LANE), jnp.bfloat16),
        ],
        in_specs=[VMEM] * 4,
        out_specs=[VMEM] * 2,
    )(own_up, own_sum, other_sum, tops)
    slots = call(
        spread_kernel,
        [jax.ShapeDtypeStruct(spread_shape, jnp.bfloat16)] * peer_count,
        in_specs=[HBM] * (4 + len(parts)),
        out_specs=[HBM] * peer_count,
        scratch_shapes=[
            pltpu.VMEM((peer_count,) + spread_shape, jnp.bfloat16),
            pltpu.VMEM((2, META, send_rows), jnp.bfloat16),
            pltpu.VMEM((len(parts), 2 * send_rows, own_rows), jnp.bfloat16),
            pltpu.SemaphoreType.DMA((4 + len(parts),)),
            pltpu.SemaphoreType.DMA((peer_count,)),
        ],
    )(own_up, mate_up, up_side, up_below, *parts)
    sent = {}
    for distance in sorted(range(1, peer_count), key=lambda d: (-bin(d >> 1).count("1"), d)):
        sent[distance] = lax.ppermute(
            slots[distance], "tok", [(t, t ^ distance) for t in range(peer_count)]
        )
    sent[0] = slots[0]
    order = list(sent)
    input_grad, gate_grad, delta_scale, delta_codes = call(
        functools.partial(finish_kernel, order=order),
        (
            jax.ShapeDtypeStruct((peer_count * cap, 2 * own_rows), jnp.bfloat16),
            jax.ShapeDtypeStruct(gate_pre.shape, jnp.bfloat16),
            jax.ShapeDtypeStruct(block_rows.shape, jnp.float32),
            jax.ShapeDtypeStruct(delta.shape, jnp.bfloat16),
        ),
        in_specs=[HBM] * (3 + peer_count),
        out_specs=(HBM,) + (VMEM,) * 3,
        scratch_shapes=[
            pltpu.VMEM(gate_pre.shape, jnp.bfloat16),
            pltpu.VMEM(hidden_grad.shape, jnp.bfloat16),
            pltpu.VMEM(delta.shape, jnp.float32),
            pltpu.VMEM((peer_count,) + spread_shape, jnp.bfloat16),
            pltpu.SemaphoreType.DMA((3 + peer_count,)),
            pltpu.SemaphoreType.DMA((peer_count,)),
        ],
    )(gate_pre, hidden_grad, new_delta, *[sent[distance] for distance in order])
    return (input_grad, gate_grad, new_delta, new_m, new_v, delta_scale, delta_codes)


def per_device(tok_size, col_size, *arrays):
    rollout, up_codes = arrays[0], arrays[3]
    fits = (
        tok_size == 8 and col_size == 4
        and rollout.shape[0] == LANE
        and up_codes.shape[0] % LANE == 0
        and up_codes.shape[1] == 2 * BLK
    )
    if fits:
        return paired(tok_size, *arrays)
    return any_mesh(*arrays)


def solution(mesh):
    placed = (
        P("tok", None),
        P("tok"),
        P("tok", None),
        P("tok", "col"),
        P(None, "col"),
        P("col", None),
        P("tok", "col", None, None),
        P("tok", "col", None, None),
        P("tok", "col", None, None),
        P("tok", "col"),
        P("tok", "col"),
    )
    return jax.shard_map(
        functools.partial(per_device, mesh.shape["tok"], mesh.shape["col"]),
        mesh=mesh,
        in_specs=placed,
        out_specs=(
            P("tok", "col"),
            P("tok", "col"),
            P("tok", "col", None, None),
            P("tok", "col", None, None),
            P("tok", "col", None, None),
            P("col", None),
            P("tok", "col", None, None),
        ),
        check_vma=False,
    )
```
